128 devices in a mesh: row: 8 (over y, x_hi), col: 16 (over x_lo, z, core).
Axes of the slice: x: 4 (x_hi: 2, x_lo: 2; x = x_hi * 2 + x_lo), y: 4, z: 4, core: 2. Of those that a mesh axis runs over, the one named last changes fastest.
Arguments:
- alignment: float32 [512, 512, 256], P('row', 'col'), may hold values from -6 to 6
- align_gain: float32 [256], replicated, may hold values from 0.5 to 1.5
- align_bias: float32 [256], replicated, may hold values from -1.75 to 1.75
- left_weight: float32 [256, 32], replicated, may hold values from -0.375 to 0.375
- right_weight: float32 [256, 32], replicated, may hold values from -0.375 to 0.375
- project_weight: float32 [1024, 128], replicated, may hold values from -3 to 3
- project_bias: float32 [128], replicated, may hold values from -1.75 to 1.75
- pair_state: float32 [512, 512, 128], P('row', 'col'), may hold values from -6 to 6
- pair_gain: float32 [128], replicated, may hold values from 0.5 to 1.5
- pair_bias: float32 [128], replicated, may hold values from -1.75 to 1.75
- hidden_weight: float32 [128, 512], replicated, may hold values from -0.5 to 0.5
- hidden_bias: float32 [512], replicated, may hold values from -1.75 to 1.75
- final_weight: float32 [512, 128], replicated, may hold values from -0.25 to 0.25
- final_bias: float32 [128], replicated, may hold values from -1.75 to 1.75
Outputs:
- pair_next: float32 [512, 512, 128], P('row', 'col')
The draws below stay inside these ranges and needn't reach their ends.
All inputs are finite; a program needn't handle non-finite values.
Results may differ from the reference program's by a relative error of at most 0.0003.
Values sent between devices are 32-bit elements; how exact they have to be, the bound alone decides.
A program may use at most 128 MiB of HBM per device.

```python
import jax
import jax.numpy as jnp
from jax import lax

CM = 256
C = 32
P_SIZE = 128
H = 512
S = 512
R = 512


def shard_levels(key, extent, pieces, least, largest):
    level, own = 1.0, jax.random.fold_in(key, 6)
    for axis_at, blocks in pieces:
        heights = jnp.exp(jax.random.uniform(jax.random.fold_in(own, axis_at), (blocks,), jnp.float32, least / len(pieces), largest / len(pieces)))
        level = level * jnp.repeat(heights, extent[axis_at] // blocks).reshape([-1 if axis == axis_at else 1 for axis in range(len(extent))])
    return level


def noise(key, dims, scale, limit, split=(), held_as=jnp.bfloat16):
    level = shard_levels(key, dims, split, -0.22, 0.18) if split else 1.0
    values = jax.random.normal(key, dims, jnp.float32) * scale * level
    return jnp.minimum(jnp.maximum(values, -limit), limit).astype(held_as)


def setup_inputs(seed: int = 0) -> dict:
    arg_keys = jax.random.split(jax.random.key(seed), 15)
    return {
        "alignment": noise(arg_keys[0], (S, R, CM), 1.0, 6.0, ((0, 8), (1, 16)), jnp.float32),
        "align_gain": jnp.clip(1.0 + 0.1 * jax.random.normal(arg_keys[1], (CM,), jnp.float32), 0.5, 1.5),
        "align_bias": noise(arg_keys[2], (CM,), 0.3, 1.75, (), jnp.float32),
        "left_weight": noise(arg_keys[3], (CM, C), CM ** -0.5, 0.375, (), jnp.float32),
        "right_weight": noise(arg_keys[4], (CM, C), CM ** -0.5, 0.375, (), jnp.float32),
        "project_weight": noise(arg_keys[5], (C * C, P_SIZE), 0.5, 3.0, (), jnp.float32),
        "project_bias": noise(arg_keys[6], (P_SIZE,), 0.3, 1.75, (), jnp.float32),
        "pair_state": noise(arg_keys[7], (R, R, P_SIZE), 1.0, 6.0, ((0, 8), (1, 16)), jnp.float32),
        "pair_gain": jnp.clip(1.0 + 0.1 * jax.random.normal(arg_keys[8], (P_SIZE,), jnp.float32), 0.5, 1.5),
        "pair_bias": noise(arg_keys[9], (P_SIZE,), 0.3, 1.75, (), jnp.float32),
        "hidden_weight": noise(arg_keys[10], (P_SIZE, H), P_SIZE ** -0.5, 0.5, (), jnp.float32),
        "hidden_bias": noise(arg_keys[11], (H,), 0.3, 1.75, (), jnp.float32),
        "final_weight": noise(arg_keys[12], (H, P_SIZE), H ** -0.5, 0.25, (), jnp.float32),
        "final_bias": noise(arg_keys[13], (P_SIZE,), 0.3, 1.75, (), jnp.float32),
    }


def layer_norm(values, gain, offset):
    middle = lax.optimization_barrier(jnp.mean(values, axis=-1, keepdims=True))
    spread = lax.optimization_barrier(jnp.mean(jnp.square(values - middle), axis=-1, keepdims=True))
    return (values - middle) * lax.rsqrt(spread + 1e-05) * gain + offset

def reference(alignment, align_gain, align_bias, left_weight, right_weight, project_weight, project_bias, pair_state, pair_gain, pair_bias, hidden_weight, hidden_bias, final_weight, final_bias):
    highest = lax.Precision.HIGHEST
    normed = layer_norm(alignment, align_gain, align_bias).reshape(S * R, CM)
    left = jnp.dot(normed, left_weight, precision=highest, preferred_element_type=jnp.float32).reshape(S, R * C)
    right = jnp.dot(normed, right_weight, precision=highest, preferred_element_type=jnp.float32).reshape(S, R * C)
    block_rows = 16

    def one_block(index):
        piece = lax.dynamic_slice_in_dim(left, (index * block_rows * C).astype(jnp.int32), block_rows * C, 1)
        product = lax.dot_general(piece, right, (((0,), (0,)), ((), ())), precision=highest, preferred_element_type=jnp.float32) / S
        product = product.reshape(block_rows, C, R, C).transpose(0, 2, 1, 3).reshape(block_rows * R, C * C)
        return jnp.dot(product, project_weight, precision=highest, preferred_element_type=jnp.float32)
    update = lax.map(one_block, jnp.arange(R // block_rows, dtype=jnp.int32)).reshape(R, R, P_SIZE)
    updated = pair_state + update + project_bias
    flat = layer_norm(updated, pair_gain, pair_bias).reshape(R * R, P_SIZE)
    hidden = jax.nn.relu(jnp.dot(flat, hidden_weight, precision=highest, preferred_element_type=jnp.float32) + hidden_bias)
    output = jnp.dot(hidden, final_weight, precision=highest, preferred_element_type=jnp.float32) + final_bias
    return updated + output.reshape(R, R, P_SIZE)
```

```python
import functools

import jax
import jax.numpy as jnp
from jax import lax
from jax.experimental import pallas as pl
from jax.experimental.pallas import tpu as pltpu
from jax.sharding import PartitionSpec as P

F32 = jnp.float32
BF16 = jnp.bfloat16
MESH = pl.DeviceIdType.MESH
CH = 4


def split(value):
    high = value.astype(BF16)
    low = (value - high.astype(F32)).astype(BF16)
    return high, low


def dot(a, b):
    return jnp.dot(a, b, preferred_element_type=F32)


def center(values, width):
    total = values[0]
    for part in values[1:]:
        total = total + part
    middle = jnp.sum(total, axis=-1, keepdims=True) * (1.0 / width)
    values = [part - middle for part in values]
    total = values[0] * values[0]
    for part in values[1:]:
        total = total + part * part
    spread = jnp.sum(total, axis=-1, keepdims=True) * (1.0 / width)
    factor = lax.rsqrt(spread + 1e-05)
    return [part * factor for part in values]


def kernel(
    align,
    gain_ref,
    offset_ref,
    lw_ref,
    rw_ref,
    pw_hbm,
    pbias_ref,
    pair_hbm,
    pgain_ref,
    poffset_ref,
    hw_ref,
    hbias_ref,
    fw_ref,
    fbias_ref,
    out_hbm,
    x0,
    x1,
    xh,
    xl,
    wh,
    wl,
    send_left,
    left,
    right,
    lhs,
    rhs,
    raw,
    oh,
    ol,
    pw,
    pwc,
    hwc,
    fwc,
    pair,
    out,
    load_sem,
    r_send,
    r_recv,
    l_send,
    l_recv,
    c_send,
    c_recv,
    t_send,
    t_recv,
    out_sem,
):
    row, col = lax.axis_index("row"), lax.axis_index("col")
    y, x_hi = row // 2, row % 2
    k, core = col // 2, col % 2
    x_lo, z = k // 4, k % 4

    def at_row(y_, x_):
        return (y_ % 4) * 2 + x_

    def at_k(x_, z_):
        return x_ * 4 + z_ % 4

    def same_col(r):
        return (r, col)

    def same_row(k_):
        return (row, k_ * 2 + core)

    other_core = (row, k * 2 + 1 - core)
    swap = (k, row * 2 + core)
    y_up, y_down = same_col(at_row(y + 1, x_hi)), same_col(at_row(y + 3, x_hi))
    x_far = same_col(at_row(y, 1 - x_hi))
    z_up, z_down = same_row(at_k(x_lo, z + 1)), same_row(at_k(x_lo, z + 3))
    x_near = same_row(at_k(1 - x_lo, z))
    stays = k == row

    loads = [
        pltpu.make_async_copy(align.at[:, pl.ds(0, 128)], x0, load_sem.at[0]),
        pltpu.make_async_copy(align.at[:, pl.ds(128, 128)], x1, load_sem.at[1]),
        pltpu.make_async_copy(pw_hbm, pw, load_sem.at[2]),
        pltpu.make_async_copy(pair_hbm, pair, load_sem.at[3]),
    ]
    for load in loads:
        load.start()

    barrier = pltpu.get_barrier_semaphore()
    for device in (other_core, y_up, y_down, x_far, z_up, z_down, x_near):
        pl.semaphore_signal(barrier, inc=1, device_id=device, device_id_type=MESH)

    @pl.when(jnp.logical_not(stays))
    def _():
        pl.semaphore_signal(barrier, inc=1, device_id=swap, device_id_type=MESH)

    lane = lax.broadcasted_iota(jnp.int32, (256, 128), 1)
    for source, at in ((lw_ref, 0), (rw_ref, 128)):
        wide = jnp.concatenate([source[...]] * 4, axis=1)
        for pos in range(4):
            placed = jnp.where(lane // 32 == pos, wide, 0.0)
            high, low = split(placed)
            wh[pl.ds(pos * 256, 256), pl.ds(at, 128)] = high
            wl[pl.ds(pos * 256, 256), pl.ds(at, 128)] = low

    loads[0].wait()
    loads[1].wait()

    gain = gain_ref[...]
    offset = offset_ref[...]

    def norm_body(g, carry):
        for pos in range(4):
            rows = pl.ds(g * 4 + pos, 64, stride=32)
            parts = center([x0[rows, :], x1[rows, :]], 256)
            for half in range(2):
                value = parts[half] * gain[:, half * 128 : half * 128 + 128] + offset[:, half * 128 : half * 128 + 128]
                high, low = split(value)
                at = pl.ds(pl.multiple_of(g * 64, 64), 64)
                xh[at, pl.ds(pos * 256 + half * 128, 128)] = high
                xl[at, pl.ds(pos * 256 + half * 128, 128)] = low
        return carry

    lax.fori_loop(0, 8, norm_body, 0)
    both = dot(xh[...], wh[...]) + dot(xl[...], wh[...]) + dot(xh[...], wl[...])
    for g in range(8):
        send_left[g // 2, :, pl.ds((g % 2) * 128, 128)] = both[g * 64 : g * 64 + 64, :128]
    for g in range(4):
        pair_rows = jnp.concatenate(
            [both[g * 64 : g * 64 + 64, 128:], both[g * 64 + 256 : g * 64 + 320, 128:]], axis=0
        )
        right[row, pl.ds(g * 128, 128), :] = pair_rows.T

    @pl.when(jnp.logical_not(stays))
    def _():
        pl.semaphore_wait(barrier, 8)

    @pl.when(stays)
    def _():
        pl.semaphore_wait(barrier, 7)

    def r_copy(step, n, slot, device):
        block = right.at[slot, pl.ds(n * 128, 128), :]
        return pltpu.make_async_remote_copy(
            src_ref=block,
            dst_ref=block,
            send_sem=r_send.at[step, n],
            recv_sem=r_recv.at[step, n],
            device_id=device,
            device_id_type=MESH,
        )

    def l_copy(step, n, slot, device):
        block = left.at[n, core, slot]
        return pltpu.make_async_remote_copy(
            src_ref=block,
            dst_ref=block,
            send_sem=l_send.at[step, n],
            recv_sem=l_recv.at[step, n],
            device_id=device,
            device_id_type=MESH,
        )

    def c_copy(step, n, slot, half):
        block = left.at[n, half, slot]
        return pltpu.make_async_remote_copy(
            src_ref=block,
            dst_ref=block,
            send_sem=c_send.at[step, n],
            recv_sem=c_recv.at[step, n],
            device_id=other_core,
            device_id_type=MESH,
        )

    def t_copy(n):
        return pltpu.make_async_remote_copy(
            src_ref=send_left.at[n],
            dst_ref=left.at[n, core, row],
            send_sem=t_send.at[n],
            recv_sem=t_recv.at[n],
            device_id=swap,
            device_id_type=MESH,
        )

    def t_arrival(n):
        return pltpu.make_async_copy(send_left.at[n], left.at[n, core, k], t_recv.at[n])

    r_sent = [row, row, row, at_row(y, 1 - x_hi), at_row(y, 1 - x_hi), at_row(y + 3, x_hi), at_row(y + 1, 1 - x_hi)]
    r_to = [x_far, y_up, y_down, y_up, y_down, y_up, y_down]
    r_lands = [
        at_row(y, 1 - x_hi),
        at_row(y + 3, x_hi),
        at_row(y + 1, x_hi),
        at_row(y + 3, 1 - x_hi),
        at_row(y + 1, 1 - x_hi),
        at_row(y + 2, x_hi),
        at_row(y + 2, 1 - x_hi),
    ]
    l_sent = [k, k, k, at_k(1 - x_lo, z), at_k(1 - x_lo, z), at_k(x_lo, z + 3), at_k(1 - x_lo, z + 1)]
    l_to = [x_near, z_up, z_down, z_up, z_down, z_up, z_down]
    l_lands = [
        at_k(1 - x_lo, z),
        at_k(x_lo, z + 3),
        at_k(x_lo, z + 1),
        at_k(1 - x_lo, z + 3),
        at_k(1 - x_lo, z + 1),
        at_k(x_lo, z + 2),
        at_k(1 - x_lo, z + 2),
    ]
    c_slots = [k] + l_lands

    def r_start(step, n):
        r_copy(step, n, r_sent[step], r_to[step]).start()

    def r_wait(step, n):
        r_copy(step, n, r_lands[step], r_to[step]).wait_recv()

    def l_start(step, n):
        l_copy(step, n, l_sent[step], l_to[step]).start()

    def l_wait(step, n):
        l_copy(step, n, l_lands[step], l_to[step]).wait_recv()

    def c_start(step, n):
        c_copy(step, n, c_slots[step], core).start()

    def c_wait(step, n):
        c_copy(step, n, c_slots[step], 1 - core).wait_recv()

    for n in range(CH):

        @pl.when(jnp.logical_not(stays))
        def _(n=n):
            t_copy(n).start()

        @pl.when(stays)
        def _(n=n):
            t_arrival(n).start()

        for step in (1, 2, 0):
            r_start(step, n)

    loads[2].wait()

    def order_body(d, carry):
        high, low = split(pw[pl.ds(d, 32, stride=32), :])
        at = pl.ds(pl.multiple_of(d * 32, 32), 32)
        pwc[at, pl.ds(0, 128)] = high
        pwc[at, pl.ds(128, 128)] = low
        return carry

    lax.fori_loop(0, 32, order_body, 0)
    high, low = split(hw_ref[...])
    hwc[pl.ds(0, 128), :] = high
    hwc[pl.ds(128, 128), :] = high
    hwc[pl.ds(256, 128), :] = low
    high, low = split(fw_ref[...])
    fwc[:, pl.ds(0, 128)] = high
    fwc[:, pl.ds(128, 128)] = low

    def wave_a(n):
        t_arrival(n).wait()
        for step in (0, 1, 2):
            l_start(step, n)
        c_start(0, n)

    def wave_b(n):
        l_wait(0, n)
        l_start(3, n)
        l_start(4, n)
        c_start(1, n)
        r_wait(0, n)
        r_start(3, n)
        r_start(4, n)

    def wave_c(n):
        r_wait(1, n)
        r_start(5, n)
        l_wait(1, n)
        l_start(5, n)
        c_start(2, n)
        l_wait(2, n)
        c_start(3, n)

    def wave_d(n):
        r_wait(4, n)
        r_start(6, n)
        l_wait(4, n)
        l_start(6, n)
        c_start(5, n)
        l_wait(3, n)
        c_start(4, n)

    def wave_e(n):
        l_wait(5, n)
        c_start(6, n)
        l_wait(6, n)
        c_start(7, n)

    waves = [wave_a, wave_b, wave_c, wave_d, wave_e]
    for turn in range(CH + len(waves) - 1):
        for at, wave in enumerate(waves):
            if 0 <= turn - at < CH:
                wave(turn - at)
    for n in range(CH):
        for step in (2, 3, 5, 6):
            r_wait(step, n)

    low_half = lax.broadcasted_iota(jnp.int32, (16, 128), 1) < 64

    def right_body(d, carry):
        first, second = [], []
        for p in range(4):
            a = right[2 * p, pl.ds(d, 16, stride=32), :]
            b = right[2 * p + 1, pl.ds(d, 16, stride=32), :]
            first.append(jnp.where(low_half, a, pltpu.roll(b, 64, 1)))
            second.append(jnp.where(low_half, pltpu.roll(a, 64, 1), b))
        for at, parts in enumerate((first, second)):
            rows = pl.ds(pl.multiple_of(d * 32 + at * 16, 16), 16)
            for p in range(4):
                high, low = split(parts[p])
                lhs[rows, pl.ds(p * 128, 128)] = high
                lhs[rows, pl.ds(512 + p * 128, 128)] = low
                lhs[rows, pl.ds(1024 + p * 128, 128)] = high
        return carry

    lax.fori_loop(0, 32, right_body, 0)
    loads[3].wait()

    lane = lax.broadcasted_iota(jnp.int32, (32, 128), 1)
    below = lane < 64
    even = (lane // 32) % 2 == 0
    pbias, fbias, hbias = pbias_ref[...], fbias_ref[...], hbias_ref[...]
    pgain, poffset = pgain_ref[...], poffset_ref[...]

    def exchange_halves(a, b):
        moved = pltpu.roll(jnp.where(below, b, a), 64, 1)
        return jnp.where(below, a, moved), jnp.where(below, moved, b)

    def exchange_quarters(a, b):
        return jnp.where(even, a, pltpu.roll(b, 32, 1)), jnp.where(even, pltpu.roll(a, 96, 1), b)

    def tile_body(m, carry):
        q, h = m // 2, m % 2
        piece = left[q, h].reshape(512, 256)
        high, low = split(piece)
        rhs[pl.ds(0, 512), :] = high
        rhs[pl.ds(512, 512), :] = high
        rhs[pl.ds(1024, 512), :] = low
        raw[...] = dot(lhs[...], rhs[...])
        for t in range(8):
            for u in range(2):
                v = [raw[pl.ds((4 * t + d) * 32, 32), pl.ds(u * 128, 128)] for d in range(4)]
                v[0], v[2] = exchange_halves(v[0], v[2])
                v[1], v[3] = exchange_halves(v[1], v[3])
                v[0], v[1] = exchange_quarters(v[0], v[1])
                v[2], v[3] = exchange_quarters(v[2], v[3])
                for i in range(4):
                    high, low = split(v[i])
                    oh[pl.ds((u * 4 + i) * 32, 32), pl.ds(t * 128, 128)] = high
                    ol[pl.ds((u * 4 + i) * 32, 32), pl.ds(t * 128, 128)] = low
        wide = dot(oh[...], pwc[...])
        update = wide[:, :128] + wide[:, 128:] + dot(ol[...], pwc[:, :128])
        rows = pl.ds(pl.multiple_of((h * 32 + q * 8) * 32, 256), 256)
        updated = pair[rows, :] + update * (1.0 / 512) + pbias
        (flat,) = center([updated], 128)
        high, low = split(flat * pgain + poffset)
        hidden = jnp.maximum(dot(jnp.concatenate([high, low, high], axis=1), hwc[...]) + hbias, 0.0)
        high, low = split(hidden)
        wide = dot(high, fwc[...])
        final = wide[:, :128] + wide[:, 128:] + dot(low, fwc[:, :128])
        out[rows, :] = updated + final + fbias
        return carry

    def step_body(m, carry):
        q, h = m // 2, m % 2

        @pl.when(h == 0)
        def _():
            for step in range(8):
                c_wait(step, q)

        tile_body(m, carry)
        rows = pl.ds(pl.multiple_of((h * 32 + q * 8) * 32, 256), 256)
        pltpu.make_async_copy(out.at[rows, :], out_hbm.at[rows, :], out_sem.at[m]).start()
        return carry

    lax.fori_loop(0, 8, step_body, 0)

    def out_wait(m, carry):
        q, h = m // 2, m % 2
        rows = pl.ds(pl.multiple_of((h * 32 + q * 8) * 32, 256), 256)
        pltpu.make_async_copy(out.at[rows, :], out_hbm.at[rows, :], out_sem.at[m]).wait()
        return carry

    lax.fori_loop(0, 8, out_wait, 0)
    for n in range(CH):
        for step in range(7):
            r_copy(step, n, r_sent[step], r_to[step]).wait_send()
            l_copy(step, n, l_sent[step], l_to[step]).wait_send()
        for step in range(8):
            c_copy(step, n, c_slots[step], core).wait_send()

        @pl.when(jnp.logical_not(stays))
        def _(n=n):
            t_copy(n).wait_send()


def on_device(
    alignment,
    align_gain,
    align_bias,
    left_weight,
    right_weight,
    project_weight,
    project_bias,
    pair_state,
    pair_gain,
    pair_bias,
    hidden_weight,
    hidden_bias,
    final_weight,
    final_bias,
):
    whole = pl.BlockSpec(memory_space=pltpu.VMEM)
    apart = pl.BlockSpec(memory_space=pl.ANY)
    dma = pltpu.SemaphoreType.DMA
    output = pl.pallas_call(
        kernel,
        out_shape=jax.ShapeDtypeStruct((2048, 128), F32),
        in_specs=[apart, whole, whole, whole, whole, apart, whole, apart] + [whole] * 6,
        out_specs=apart,
        scratch_shapes=[
            pltpu.VMEM((2048, 128), F32),
            pltpu.VMEM((2048, 128), F32),
            pltpu.VMEM((512, 1024), BF16),
            pltpu.VMEM((512, 1024), BF16),
            pltpu.VMEM((1024, 256), BF16),
            pltpu.VMEM((1024, 256), BF16),
            pltpu.VMEM((CH, 64, 256), F32),
            pltpu.VMEM((CH, 2, 8, 64, 256), F32),
            pltpu.VMEM((8, 512, 128), F32),
            pltpu.VMEM((1024, 1536), BF16),
            pltpu.VMEM((1536, 256), BF16),
            pltpu.VMEM((1024, 256), F32),
            pltpu.VMEM((256, 1024), BF16),
            pltpu.VMEM((256, 1024), BF16),
            pltpu.VMEM((1024, 128), F32),
            pltpu.VMEM((1024, 256), BF16),
            pltpu.VMEM((384, 512), BF16),
            pltpu.VMEM((512, 256), BF16),
            pltpu.VMEM((2048, 128), F32),
            pltpu.VMEM((2048, 128), F32),
            dma((4,)),
            dma((7, CH)),
            dma((7, CH)),
            dma((7, CH)),
            dma((7, CH)),
            dma((8, CH)),
            dma((8, CH)),
            dma((CH,)),
            dma((CH,)),
            dma((8,)),
        ],
        compiler_params=pltpu.CompilerParams(
            collective_id=0, has_side_effects=True, vmem_limit_bytes=48 * 1024 * 1024
        ),
        cost_estimate=pl.CostEstimate(flops=10**10, bytes_accessed=6 * 10**6, transcendentals=0),
    )(
        alignment.reshape(2048, 256),
        align_gain.reshape(1, 256),
        align_bias.reshape(1, 256),
        left_weight,
        right_weight,
        project_weight,
        project_bias.reshape(1, 128),
        pair_state.reshape(2048, 128),
        pair_gain.reshape(1, 128),
        pair_bias.reshape(1, 128),
        hidden_weight,
        hidden_bias.reshape(1, 512),
        final_weight,
        final_bias.reshape(1, 128),
    )
    return output.reshape(64, 32, 128)


def solution(mesh):
    spread = P("row", "col", None)
    placed = (spread,) + (P(),) * 6 + (spread,) + (P(),) * 6
    return jax.shard_map(on_device, mesh=mesh, in_specs=placed, out_specs=spread, check_vma=False)
```

```python
import functools

import jax
import jax.numpy as jnp
from jax import lax
from jax.experimental import pallas as pl
from jax.experimental.pallas import tpu as pltpu
from jax.sharding import PartitionSpec as P

F32 = jnp.float32
BF16 = jnp.bfloat16
MESH = pl.DeviceIdType.MESH
CH = 4
ORDER = (
    ("r1", 0), ("t1", 0), ("r0", 0), ("r1", 1), ("t1", 1), ("r0", 1), ("r1", 2), ("t1", 2), ("r0", 2),
    ("r1", 3), ("t2", 0), ("t1", 3), ("r0", 3), ("P", 0), ("t2", 1), ("r4", 0), ("t2", 2), ("r4", 1),
    ("l1", 0), ("l2", 0), ("l0", 0), ("t2", 3), ("r4", 2), ("l1", 1), ("l2", 1), ("l0", 1), ("l1", 2),
    ("l2", 2), ("l0", 2), ("r4", 3), ("P", 2), ("l5", 0), ("l4", 0), ("l0", 3), ("l3", 0), ("l2", 3),
    ("l1", 3), ("l4", 1), ("l5", 1), ("l4", 2), ("P", 1), ("P", 3), ("l3", 1), ("l6", 0), ("l5", 2),
    ("l4", 3), ("O", 0), ("l3", 2), ("l6", 1), ("F", 0), ("l3", 3), ("l6", 2), ("l5", 3), ("l6", 3), ("O", 1),
    ("F", 1), ("O", 2), ("F", 2), ("O", 3), ("F", 3),
)


def split(value):
    high = value.astype(BF16)
    low = (value - high.astype(F32)).astype(BF16)
    return high, low


def dot(a, b):
    return jnp.dot(a, b, preferred_element_type=F32)


def center(values, width):
    total = values[0]
    for part in values[1:]:
        total = total + part
    middle = jnp.sum(total, axis=-1, keepdims=True) * (1.0 / width)
    values = [part - middle for part in values]
    total = values[0] * values[0]
    for part in values[1:]:
        total = total + part * part
    spread = jnp.sum(total, axis=-1, keepdims=True) * (1.0 / width)
    factor = lax.rsqrt(spread + 1e-05)
    return [part * factor for part in values]


def kernel(
    align,
    gain_hbm,
    offset_hbm,
    lw_hbm,
    rw_hbm,
    pw_hbm,
    pbias_hbm,
    pair_hbm,
    pgain_hbm,
    poffset_hbm,
    hw_hbm,
    hbias_hbm,
    fw_hbm,
    fbias_hbm,
    out_hbm,
    gain_ref,
    offset_ref,
    lw_ref,
    rw_ref,
    pbias_ref,
    pgain_ref,
    poffset_ref,
    hw_ref,
    hbias_ref,
    fw_ref,
    fbias_ref,
    x0,
    x1,
    xh,
    xl,
    wh,
    wl,
    send_left,
    passing,
    left,
    right,
    lhs,
    rhs,
    raw,
    oh,
    ol,
    pw,
    pwc,
    hwc,
    fwc,
    pair,
    out,
    load_sem,
    r_send,
    r_recv,
    l_send,
    l_recv,
    c_send,
    c_recv,
    t_send,
    t_recv,
    out_sem,
):
    row, col = lax.axis_index("row"), lax.axis_index("col")
    y, x_hi = row // 2, row % 2
    k, core = col // 2, col % 2
    x_lo, z = k // 4, k % 4

    def at_row(y_, x_):
        return (y_ % 4) * 2 + x_

    def at_k(x_, z_):
        return x_ * 4 + z_ % 4

    def same_col(r):
        return (r, col)

    def same_row(k_):
        return (row, k_ * 2 + core)

    other_core = (row, k * 2 + 1 - core)
    t_y = 2 * x_lo + z // 2
    t_x = jnp.where(x_hi == z % 2, x_lo, 1 - x_lo)
    t_z = (z + y - t_y + 4) % 4
    first_to = (y * 2 + z % 2, (t_x * 4 + t_z) * 2 + core)
    mid = (z - y - x_hi + 8) % 4
    mid_x, mid_w = mid // 2, mid % 2
    mid_hi = jnp.where(x_lo == mid_x, x_hi, 1 - x_hi)
    first_from = (y * 2 + mid_hi, (mid_x * 4 + 2 * mid_w + x_hi) * 2 + core)
    mid_shard = y * 2 + mid_hi
    mid_y = 2 * mid_x + mid_w
    second_to = (mid_y * 2 + x_hi, col)

    def shard_at(x_, z_):
        return ((z_ - y % 2 - x_hi + 2 * (y // 2) + 8) % 4) * 2 + jnp.where(x_ == y // 2, x_hi, 1 - x_hi)

    shard = shard_at(x_lo, z)
    second_from = ((shard // 2) * 2 + x_hi, col)
    here_first = jnp.logical_and(first_to[0] == row, first_to[1] == col)
    here_second = mid_y == y
    y_up, y_down = same_col(at_row(y + 1, x_hi)), same_col(at_row(y + 3, x_hi))
    x_far = same_col(at_row(y, 1 - x_hi))
    z_up, z_down = same_row(at_k(x_lo, z + 1)), same_row(at_k(x_lo, z + 3))
    x_near = same_row(at_k(1 - x_lo, z))

    moves = [
        (lw_hbm, lw_ref),
        (rw_hbm, rw_ref),
        (align.at[:, pl.ds(0, 128)], x0),
        (align.at[:, pl.ds(128, 128)], x1),
        (gain_hbm, gain_ref),
        (offset_hbm, offset_ref),
        (pw_hbm, pw),
        (hw_hbm, hw_ref),
        (fw_hbm, fw_ref),
        (pair_hbm, pair),
        (pbias_hbm, pbias_ref),
        (pgain_hbm, pgain_ref),
        (poffset_hbm, poffset_ref),
        (hbias_hbm, hbias_ref),
        (fbias_hbm, fbias_ref),
    ]
    loads = [pltpu.make_async_copy(source, target, load_sem.at[at]) for at, (source, target) in enumerate(moves)]
    for load in loads:
        load.start()

    barrier = pltpu.get_barrier_semaphore()
    for device in (other_core, y_up, y_down, x_far, z_up, z_down, x_near):
        pl.semaphore_signal(barrier, inc=1, device_id=device, device_id_type=MESH)

    for device in (first_from, second_from):

        @pl.when(jnp.logical_or(device[0] != row, device[1] != col))
        def _(device=device):
            pl.semaphore_signal(barrier, inc=1, device_id=device, device_id_type=MESH)

    lane = lax.broadcasted_iota(jnp.int32, (256, 128), 1)
    loads[0].wait()
    loads[1].wait()
    for source, at in ((lw_ref, 0), (rw_ref, 128)):
        wide = jnp.concatenate([source[...]] * 4, axis=0).T
        for pos in range(4):
            placed = jnp.where(lane // 32 == pos, wide, 0.0)
            high, low = split(placed)
            wh[pl.ds(pos * 256, 256), pl.ds(at, 128)] = high
            wl[pl.ds(pos * 256, 256), pl.ds(at, 128)] = low

    for at in range(2, 6):
        loads[at].wait()

    gain = gain_ref[...]
    offset = offset_ref[...]

    def norm_body(g, carry):
        for pos in range(4):
            rows = pl.ds(g * 4 + pos, 64, stride=32)
            parts = center([x0[rows, :], x1[rows, :]], 256)
            for half in range(2):
                value = parts[half] * gain[:, half * 128 : half * 128 + 128] + offset[:, half * 128 : half * 128 + 128]
                high, low = split(value)
                at = pl.ds(pl.multiple_of(g * 64, 64), 64)
                xh[at, pl.ds(pos * 256 + half * 128, 128)] = high
                xl[at, pl.ds(pos * 256 + half * 128, 128)] = low
        return carry

    lax.fori_loop(0, 8, norm_body, 0)
    both = dot(xh[...], wh[...]) + dot(xl[...], wh[...]) + dot(xh[...], wl[...])
    for g in range(8):
        send_left[g // 2, :, pl.ds((g % 2) * 128, 128)] = both[g * 64 : g * 64 + 64, :128]
    for g in range(4):
        pair_rows = jnp.concatenate(
            [both[g * 64 : g * 64 + 64, 128:], both[g * 64 + 256 : g * 64 + 320, 128:]], axis=0
        )
        right[row, pl.ds(g * 128, 128), :] = pair_rows.T

    greeted = 7 + jnp.where(here_first, 0, 1) + jnp.where(here_second, 0, 1)
    pl.semaphore_wait(barrier, greeted)

    def r_copy(step, n, slot, device):
        block = right.at[slot, pl.ds(n * 128, 128), :]
        return pltpu.make_async_remote_copy(
            src_ref=block,
            dst_ref=block,
            send_sem=r_send.at[step, n],
            recv_sem=r_recv.at[step, n],
            device_id=device,
            device_id_type=MESH,
        )

    def l_copy(step, n, slot, device):
        block = left.at[n, core, slot]
        return pltpu.make_async_remote_copy(
            src_ref=block,
            dst_ref=block,
            send_sem=l_send.at[step, n],
            recv_sem=l_recv.at[step, n],
            device_id=device,
            device_id_type=MESH,
        )

    def c_copy(step, n, slot, half):
        block = left.at[n, half, slot]
        return pltpu.make_async_remote_copy(
            src_ref=block,
            dst_ref=block,
            send_sem=c_send.at[step, n],
            recv_sem=c_recv.at[step, n],
            device_id=other_core,
            device_id_type=MESH,
        )

    def first_copy(n):
        return pltpu.make_async_remote_copy(
            src_ref=send_left.at[n],
            dst_ref=passing.at[n],
            send_sem=t_send.at[0, n],
            recv_sem=t_recv.at[0, n],
            device_id=first_to,
            device_id_type=MESH,
        )

    def second_copy(n):
        return pltpu.make_async_remote_copy(
            src_ref=passing.at[n],
            dst_ref=left.at[n, core, mid_shard],
            send_sem=t_send.at[1, n],
            recv_sem=t_recv.at[1, n],
            device_id=second_to,
            device_id_type=MESH,
        )

    def first_arrival(n):
        return pltpu.make_async_copy(send_left.at[n], passing.at[n], t_recv.at[0, n])

    def second_arrival(n):
        return pltpu.make_async_copy(passing.at[n], left.at[n, core, shard], t_recv.at[1, n])

    def t_begin(n):
        @pl.when(jnp.logical_not(here_first))
        def _():
            first_copy(n).start()

        @pl.when(here_first)
        def _():
            first_arrival(n).start()

    def t_pass(n):
        first_arrival(n).wait()

        @pl.when(jnp.logical_not(here_second))
        def _():
            second_copy(n).start()

        @pl.when(here_second)
        def _():
            second_arrival(n).start()

    r_sent = [row, row, row, at_row(y, 1 - x_hi), at_row(y, 1 - x_hi), at_row(y + 3, x_hi), at_row(y + 1, 1 - x_hi)]
    r_to = [x_far, y_up, y_down, y_up, y_down, y_up, y_down]
    r_lands = [
        at_row(y, 1 - x_hi),
        at_row(y + 3, x_hi),
        at_row(y + 1, x_hi),
        at_row(y + 3, 1 - x_hi),
        at_row(y + 1, 1 - x_hi),
        at_row(y + 2, x_hi),
        at_row(y + 2, 1 - x_hi),
    ]
    x_other = 1 - x_lo
    l_sent = [
        shard,
        shard,
        shard,
        shard_at(x_other, z),
        shard_at(x_other, z),
        shard_at(x_lo, z + 3),
        shard_at(x_other, z + 1),
    ]
    l_to = [x_near, z_up, z_down, z_up, z_down, z_up, z_down]
    l_lands = [
        shard_at(x_other, z),
        shard_at(x_lo, z + 3),
        shard_at(x_lo, z + 1),
        shard_at(x_other, z + 3),
        shard_at(x_other, z + 1),
        shard_at(x_lo, z + 2),
        shard_at(x_other, z + 2),
    ]
    c_slots = [shard] + l_lands

    def r_start(step, n):
        r_copy(step, n, r_sent[step], r_to[step]).start()

    def r_wait(step, n):
        r_copy(step, n, r_lands[step], r_to[step]).wait_recv()

    def l_start(step, n):
        l_copy(step, n, l_sent[step], l_to[step]).start()

    def l_wait(step, n):
        l_copy(step, n, l_lands[step], l_to[step]).wait_recv()

    def c_start(step, n):
        c_copy(step, n, c_slots[step], core).start()

    def c_wait(step, n):
        c_copy(step, n, c_slots[step], 1 - core).wait_recv()

    def r_first(n):
        for step in (1, 2, 0):
            r_start(step, n)

    for n in range(CH):
        t_begin(n)
        r_first(n)

    for at in range(6, 9):
        loads[at].wait()

    def order_body(d, carry):
        high, low = split(pw[pl.ds(d, 32, stride=32), :])
        at = pl.ds(pl.multiple_of(d * 32, 32), 32)
        pwc[at, pl.ds(0, 128)] = high
        pwc[at, pl.ds(128, 128)] = low
        return carry

    lax.fori_loop(0, 32, order_body, 0)
    high, low = split(hw_ref[...])
    hwc[pl.ds(0, 128), :] = high
    hwc[pl.ds(128, 128), :] = high
    hwc[pl.ds(256, 128), :] = low
    high, low = split(fw_ref[...])
    fwc[:, pl.ds(0, 128)] = high
    fwc[:, pl.ds(128, 128)] = low

    def swap_first(n):
        t_pass(n)

    def swap_second(n):
        second_arrival(n).wait()
        for step in (1, 2, 0):
            l_start(step, n)
        c_start(0, n)

    def right_relay(step, further):
        def relay(n):
            r_wait(step, n)
            for later in further:
                r_start(later, n)

        return relay

    def left_relay(step, further):
        def relay(n):
            l_wait(step, n)
            for later in further:
                l_start(later, n)
            c_start(step + 1, n)

        return relay

    low_half = lax.broadcasted_iota(jnp.int32, (16, 128), 1) < 64

    def prepare(part):
        for n in range(CH):
            for step in ((), (3,), (2,), (5, 6))[part]:
                r_wait(step, n)
        p = (y + (0, 3, 1, 2)[part]) % 4

        def body(d, carry):
            a = right[2 * p, pl.ds(d, 16, stride=32), :]
            b = right[2 * p + 1, pl.ds(d, 16, stride=32), :]
            first = jnp.where(low_half, a, pltpu.roll(b, 64, 1))
            second = jnp.where(low_half, pltpu.roll(a, 64, 1), b)
            rows = pl.ds(pl.multiple_of(d * 32, 32), 32)
            high, low = split(jnp.concatenate([first, second], axis=0))
            lhs[rows, pl.ds(pl.multiple_of(p * 128, 128), 128)] = high
            lhs[rows, pl.ds(pl.multiple_of(512 + p * 128, 128), 128)] = low
            lhs[rows, pl.ds(pl.multiple_of(1024 + p * 128, 128), 128)] = high
            return carry

        lax.fori_loop(0, 32, body, 0, unroll=4)

    for at in range(9, 15):
        loads[at].wait()

    lane = lax.broadcasted_iota(jnp.int32, (32, 128), 1)
    below = lane < 64
    even = (lane // 32) % 2 == 0
    pbias, fbias, hbias = pbias_ref[...], fbias_ref[...], hbias_ref[...]
    pgain, poffset = pgain_ref[...], poffset_ref[...]

    def exchange_halves(a, b):
        moved = pltpu.roll(jnp.where(below, b, a), 64, 1)
        return jnp.where(below, a, moved), jnp.where(below, moved, b)

    def exchange_quarters(a, b):
        return jnp.where(even, a, pltpu.roll(b, 32, 1)), jnp.where(even, pltpu.roll(a, 96, 1), b)

    def outer(q):
        for h in range(2):
            high, low = split(left[q, h].reshape(512, 256))
            at = pl.ds(h * 256, 256)
            rhs[pl.ds(0, 512), at] = high
            rhs[pl.ds(512, 512), at] = high
            rhs[pl.ds(1024, 512), at] = low
        raw[q % 2] = dot(lhs[...], rhs[...])

    def finish(q):
        for t in range(8):
            for u in range(4):
                v = [raw[q % 2, pl.ds((4 * t + d) * 32, 32), pl.ds(u * 128, 128)] for d in range(4)]
                v[0], v[2] = exchange_halves(v[0], v[2])
                v[1], v[3] = exchange_halves(v[1], v[3])
                v[0], v[1] = exchange_quarters(v[0], v[1])
                v[2], v[3] = exchange_quarters(v[2], v[3])
                for i in range(4):
                    high, low = split(v[i])
                    oh[pl.ds((u * 4 + i) * 32, 32), pl.ds(t * 128, 128)] = high
                    ol[pl.ds((u * 4 + i) * 32, 32), pl.ds(t * 128, 128)] = low
        wide = dot(oh[...], pwc[...])
        update = wide[:, :128] + wide[:, 128:] + dot(ol[...], pwc[:, :128])
        tiles = [pl.ds((h * 32 + q * 8) * 32, 256) for h in range(2)]
        updated = jnp.concatenate([pair[rows, :] for rows in tiles], axis=0) + update * (1.0 / 512) + pbias
        (flat,) = center([updated], 128)
        high, low = split(flat * pgain + poffset)
        hidden = jnp.maximum(dot(jnp.concatenate([high, low, high], axis=1), hwc[...]) + hbias, 0.0)
        high, low = split(hidden)
        wide = dot(high, fwc[...])
        final = wide[:, :128] + wide[:, 128:] + dot(low, fwc[:, :128])
        result = updated + final + fbias
        for h in range(2):
            out[tiles[h], :] = result[h * 256 : h * 256 + 256]

    def store(q, h):
        rows = pl.ds(pl.multiple_of((h * 32 + q * 8) * 32, 256), 256)
        return pltpu.make_async_copy(out.at[rows, :], out_hbm.at[rows, :], out_sem.at[q * 2 + h])

    def arrive(q):
        for step in range(8):
            c_wait(step, q)

    def product(q):
        arrive(q)
        outer(q)

    def complete(q):
        finish(q)
        store(q, 0).start()
        store(q, 1).start()

    work = {
        "t1": swap_first,
        "t2": swap_second,
        "r0": right_relay(0, (3, 4)),
        "r1": right_relay(1, (5,)),
        "r4": right_relay(4, (6,)),
        "l0": left_relay(0, (3, 4)),
        "l1": left_relay(1, (5,)),
        "l2": left_relay(2, ()),
        "l3": left_relay(3, ()),
        "l4": left_relay(4, (6,)),
        "l5": left_relay(5, ()),
        "l6": left_relay(6, ()),
        "P": prepare,
        "O": product,
        "F": complete,
    }
    for name, n in ORDER:
        work[name](n)
    for n in range(CH):
        store(n, 0).wait()
        store(n, 1).wait()
    for n in range(CH):
        for step in range(7):
            r_copy(step, n, r_sent[step], r_to[step]).wait_send()
            l_copy(step, n, l_sent[step], l_to[step]).wait_send()
        for step in range(8):
            c_copy(step, n, c_slots[step], core).wait_send()

        @pl.when(jnp.logical_not(here_first))
        def _(n=n):
            first_copy(n).wait_send()

        @pl.when(jnp.logical_not(here_second))
        def _(n=n):
            second_copy(n).wait_send()


def on_device(
    alignment,
    align_gain,
    align_bias,
    left_weight,
    right_weight,
    project_weight,
    project_bias,
    pair_state,
    pair_gain,
    pair_bias,
    hidden_weight,
    hidden_bias,
    final_weight,
    final_bias,
):
    apart = pl.BlockSpec(memory_space=pl.ANY)
    dma = pltpu.SemaphoreType.DMA
    output = pl.pallas_call(
        kernel,
        out_shape=jax.ShapeDtypeStruct((2048, 128), F32),
        in_specs=[apart] * 14,
        out_specs=apart,
        scratch_shapes=[
            pltpu.VMEM((1, 256), F32),
            pltpu.VMEM((1, 256), F32),
            pltpu.VMEM((32, 256), F32),
            pltpu.VMEM((32, 256), F32),
            pltpu.VMEM((1, 128), F32),
            pltpu.VMEM((1, 128), F32),
            pltpu.VMEM((1, 128), F32),
            pltpu.VMEM((128, 512), F32),
            pltpu.VMEM((1, 512), F32),
            pltpu.VMEM((512, 128), F32),
            pltpu.VMEM((1, 128), F32),
            pltpu.VMEM((2048, 128), F32),
            pltpu.VMEM((2048, 128), F32),
            pltpu.VMEM((512, 1024), BF16),
            pltpu.VMEM((512, 1024), BF16),
            pltpu.VMEM((1024, 256), BF16),
            pltpu.VMEM((1024, 256), BF16),
            pltpu.VMEM((CH, 64, 256), F32),
            pltpu.VMEM((CH, 64, 256), F32),
            pltpu.VMEM((CH, 2, 8, 64, 256), F32),
            pltpu.VMEM((8, 512, 128), F32),
            pltpu.VMEM((1024, 1536), BF16),
            pltpu.VMEM((1536, 512), BF16),
            pltpu.VMEM((2, 1024, 512), F32),
            pltpu.VMEM((512, 1024), BF16),
            pltpu.VMEM((512, 1024), BF16),
            pltpu.VMEM((1024, 128), F32),
            pltpu.VMEM((1024, 256), BF16),
            pltpu.VMEM((384, 512), BF16),
            pltpu.VMEM((512, 256), BF16),
            pltpu.VMEM((2048, 128), F32),
            pltpu.VMEM((2048, 128), F32),
            dma((15,)),
            dma((7, CH)),
            dma((7, CH)),
            dma((7, CH)),
            dma((7, CH)),
            dma((8, CH)),
            dma((8, CH)),
            dma((2, CH)),
            dma((2, CH)),
            dma((8,)),
        ],
        compiler_params=pltpu.CompilerParams(
            collective_id=0, has_side_effects=True, vmem_limit_bytes=63 * 1024 * 1024
        ),
        cost_estimate=pl.CostEstimate(flops=10**10, bytes_accessed=6 * 10**6, transcendentals=0),
    )(
        alignment.reshape(2048, 256),
        align_gain.reshape(1, 256),
        align_bias.reshape(1, 256),
        left_weight.T,
        right_weight.T,
        project_weight,
        project_bias.reshape(1, 128),
        pair_state.reshape(2048, 128),
        pair_gain.reshape(1, 128),
        pair_bias.reshape(1, 128),
        hidden_weight,
        hidden_bias.reshape(1, 512),
        final_weight,
        final_bias.reshape(1, 128),
    )
    return output.reshape(64, 32, 128)


def solution(mesh):
    spread = P("row", "col", None)
    placed = (spread,) + (P(),) * 6 + (spread,) + (P(),) * 6
    return jax.shard_map(on_device, mesh=mesh, in_specs=placed, out_specs=spread, check_vma=False)
```

```python
import functools

import jax
import jax.numpy as jnp
from jax import lax
from jax.experimental import pallas as pl
from jax.experimental.pallas import tpu as pltpu
from jax.sharding import PartitionSpec as P

F32 = jnp.float32
BF16 = jnp.bfloat16
MESH = pl.DeviceIdType.MESH
CH = 4
ORDER = (
    ("r0", 0), ("t1", 0), ("t1", 2), ("t1", 1), ("r0", 1), ("r0", 2), ("r0", 3), ("P", 0), ("t1", 3),
    ("r1", 0), ("t2", 0), ("t2", 2), ("r1", 2), ("r4", 0), ("r1", 1), ("t2", 1), ("r4", 2), ("l0", 0),
    ("l0", 2), ("r1", 3), ("r4", 3), ("r4", 1), ("l1", 0), ("l0", 1), ("l2", 2), ("l2", 0), ("l4", 0),
    ("t2", 3), ("l3", 0), ("P", 2), ("P", 1), ("l1", 2), ("l1", 1), ("l5", 0), ("l4", 2), ("P", 3), ("l2", 1),
    ("l3", 2), ("l6", 0), ("l4", 1), ("l3", 1), ("l0", 3), ("O", 0), ("F", 0), ("l5", 1), ("l6", 1),
    ("l6", 2), ("l3", 3), ("l1", 3), ("l2", 3), ("l4", 3), ("l5", 2), ("O", 1), ("F", 1), ("l5", 3),
    ("l6", 3), ("O", 2), ("F", 2), ("O", 3), ("F", 3),
)


def split(value):
    high = value.astype(BF16)
    low = (value - high.astype(F32)).astype(BF16)
    return high, low


def dot(a, b):
    return jnp.dot(a, b, preferred_element_type=F32)


def center(values, width):
    total = values[0]
    for part in values[1:]:
        total = total + part
    middle = jnp.sum(total, axis=-1, keepdims=True) * (1.0 / width)
    values = [part - middle for part in values]
    total = values[0] * values[0]
    for part in values[1:]:
        total = total + part * part
    spread = jnp.sum(total, axis=-1, keepdims=True) * (1.0 / width)
    factor = lax.rsqrt(spread + 1e-05)
    return [part * factor for part in values]


def kernel(
    align,
    gain_hbm,
    offset_hbm,
    lw_hbm,
    rw_hbm,
    pw_hbm,
    pbias_hbm,
    pair_hbm,
    pgain_hbm,
    poffset_hbm,
    hw_hbm,
    hbias_hbm,
    fw_hbm,
    fbias_hbm,
    out_hbm,
    gain_ref,
    offset_ref,
    lw_ref,
    rw_ref,
    pbias_ref,
    pgain_ref,
    poffset_ref,
    hw_ref,
    hbias_ref,
    fw_ref,
    fbias_ref,
    x0,
    x1,
    xh,
    xl,
    wh,
    wl,
    send_left,
    passing,
    left,
    right,
    lhs,
    rhs,
    raw,
    oh,
    ol,
    pw,
    pwc,
    hwc,
    fwc,
    pair,
    out,
    load_sem,
    r_send,
    r_recv,
    l_send,
    l_recv,
    c_send,
    c_recv,
    t_send,
    t_recv,
    out_sem,
):
    row, col = lax.axis_index("row"), lax.axis_index("col")
    y, x_hi = row // 2, row % 2
    k, core = col // 2, col % 2
    x_lo, z = k // 4, k % 4

    def at_row(y_, x_):
        return (y_ % 4) * 2 + x_

    def at_k(x_, z_):
        return x_ * 4 + z_ % 4

    def same_col(r):
        return (r, col)

    def same_row(k_):
        return (row, k_ * 2 + core)

    other_core = (row, k * 2 + 1 - core)
    t_y = 2 * x_lo + z // 2
    t_x = jnp.where(x_hi == z % 2, x_lo, 1 - x_lo)
    t_z = (z + y - t_y + 4) % 4
    first_to = (y * 2 + z % 2, (t_x * 4 + t_z) * 2 + core)
    mid = (z - y - x_hi + 8) % 4
    mid_x, mid_w = mid // 2, mid % 2
    mid_hi = jnp.where(x_lo == mid_x, x_hi, 1 - x_hi)
    first_from = (y * 2 + mid_hi, (mid_x * 4 + 2 * mid_w + x_hi) * 2 + core)
    mid_shard = y * 2 + mid_hi
    mid_y = 2 * mid_x + mid_w
    second_to = (mid_y * 2 + x_hi, col)

    def shard_at(x_, z_):
        return ((z_ - y % 2 - x_hi + 2 * (y // 2) + 8) % 4) * 2 + jnp.where(x_ == y // 2, x_hi, 1 - x_hi)

    shard = shard_at(x_lo, z)
    second_from = ((shard // 2) * 2 + x_hi, col)
    here_first = jnp.logical_and(first_to[0] == row, first_to[1] == col)
    here_second = mid_y == y
    y_up, y_down = same_col(at_row(y + 1, x_hi)), same_col(at_row(y + 3, x_hi))
    x_far = same_col(at_row(y, 1 - x_hi))
    z_up, z_down = same_row(at_k(x_lo, z + 1)), same_row(at_k(x_lo, z + 3))
    x_near = same_row(at_k(1 - x_lo, z))

    moves = [
        (lw_hbm, lw_ref),
        (rw_hbm, rw_ref),
        (align.at[:, pl.ds(0, 128)], x0),
        (align.at[:, pl.ds(128, 128)], x1),
        (gain_hbm, gain_ref),
        (offset_hbm, offset_ref),
        (pw_hbm, pw),
        (hw_hbm, hw_ref),
        (fw_hbm, fw_ref),
        (pair_hbm, pair),
        (pbias_hbm, pbias_ref),
        (pgain_hbm, pgain_ref),
        (poffset_hbm, poffset_ref),
        (hbias_hbm, hbias_ref),
        (fbias_hbm, fbias_ref),
    ]
    loads = [pltpu.make_async_copy(source, target, load_sem.at[at]) for at, (source, target) in enumerate(moves)]
    for load in loads:
        load.start()

    barrier = pltpu.get_barrier_semaphore()
    for device in (other_core, y_up, y_down, x_far, z_up, z_down, x_near):
        pl.semaphore_signal(barrier, inc=1, device_id=device, device_id_type=MESH)

    for device in (first_from, second_from):

        @pl.when(jnp.logical_or(device[0] != row, device[1] != col))
        def _(device=device):
            pl.semaphore_signal(barrier, inc=1, device_id=device, device_id_type=MESH)

    lane = lax.broadcasted_iota(jnp.int32, (256, 128), 1)
    loads[0].wait()
    loads[1].wait()
    for source, at in ((lw_ref, 0), (rw_ref, 128)):
        wide = jnp.concatenate([source[...]] * 4, axis=0).T
        for pos in range(4):
            placed = jnp.where(lane // 32 == pos, wide, 0.0)
            high, low = split(placed)
            wh[pl.ds(pos * 256, 256), pl.ds(at, 128)] = high
            wl[pl.ds(pos * 256, 256), pl.ds(at, 128)] = low

    for at in range(2, 6):
        loads[at].wait()

    gain = gain_ref[...]
    offset = offset_ref[...]

    def r_copy(step, n, slot, device):
        block = right.at[slot, pl.ds(n * 128, 128), :]
        return pltpu.make_async_remote_copy(
            src_ref=block,
            dst_ref=block,
            send_sem=r_send.at[step, n],
            recv_sem=r_recv.at[step, n],
            device_id=device,
            device_id_type=MESH,
        )

    def l_copy(step, n, slot, device):
        block = left.at[n, core, slot]
        return pltpu.make_async_remote_copy(
            src_ref=block,
            dst_ref=block,
            send_sem=l_send.at[step, n],
            recv_sem=l_recv.at[step, n],
            device_id=device,
            device_id_type=MESH,
        )

    def c_copy(step, n, slot, half):
        block = left.at[n, half, slot]
        return pltpu.make_async_remote_copy(
            src_ref=block,
            dst_ref=block,
            send_sem=c_send.at[step, n],
            recv_sem=c_recv.at[step, n],
            device_id=other_core,
            device_id_type=MESH,
        )

    def first_copy(n):
        return pltpu.make_async_remote_copy(
            src_ref=send_left.at[n],
            dst_ref=passing.at[n],
            send_sem=t_send.at[0, n],
            recv_sem=t_recv.at[0, n],
            device_id=first_to,
            device_id_type=MESH,
        )

    def second_copy(n):
        return pltpu.make_async_remote_copy(
            src_ref=passing.at[n],
            dst_ref=left.at[n, core, mid_shard],
            send_sem=t_send.at[1, n],
            recv_sem=t_recv.at[1, n],
            device_id=second_to,
            device_id_type=MESH,
        )

    def first_arrival(n):
        return pltpu.make_async_copy(send_left.at[n], passing.at[n], t_recv.at[0, n])

    def second_arrival(n):
        return pltpu.make_async_copy(passing.at[n], left.at[n, core, shard], t_recv.at[1, n])

    def t_begin(n):
        @pl.when(jnp.logical_not(here_first))
        def _():
            first_copy(n).start()

        @pl.when(here_first)
        def _():
            first_arrival(n).start()

    def t_pass(n):
        first_arrival(n).wait()

        @pl.when(jnp.logical_not(here_second))
        def _():
            second_copy(n).start()

        @pl.when(here_second)
        def _():
            second_arrival(n).start()

    r_sent = [row, row, row, at_row(y, 1 - x_hi), at_row(y, 1 - x_hi), at_row(y + 3, x_hi), at_row(y + 1, 1 - x_hi)]
    r_to = [x_far, y_up, y_down, y_up, y_down, y_up, y_down]
    r_lands = [
        at_row(y, 1 - x_hi),
        at_row(y + 3, x_hi),
        at_row(y + 1, x_hi),
        at_row(y + 3, 1 - x_hi),
        at_row(y + 1, 1 - x_hi),
        at_row(y + 2, x_hi),
        at_row(y + 2, 1 - x_hi),
    ]
    x_other = 1 - x_lo
    l_sent = [
        shard,
        shard,
        shard,
        shard_at(x_other, z),
        shard_at(x_other, z),
        shard_at(x_lo, z + 3),
        shard_at(x_other, z + 1),
    ]
    l_to = [x_near, z_up, z_down, z_up, z_down, z_up, z_down]
    l_lands = [
        shard_at(x_other, z),
        shard_at(x_lo, z + 3),
        shard_at(x_lo, z + 1),
        shard_at(x_other, z + 3),
        shard_at(x_other, z + 1),
        shard_at(x_lo, z + 2),
        shard_at(x_other, z + 2),
    ]
    c_slots = [shard] + l_lands

    def r_start(step, n):
        r_copy(step, n, r_sent[step], r_to[step]).start()

    def r_wait(step, n):
        r_copy(step, n, r_lands[step], r_to[step]).wait_recv()

    def l_start(step, n):
        l_copy(step, n, l_sent[step], l_to[step]).start()

    def l_wait(step, n):
        l_copy(step, n, l_lands[step], l_to[step]).wait_recv()

    def c_start(step, n):
        c_copy(step, n, c_slots[step], core).start()

    def c_wait(step, n):
        c_copy(step, n, c_slots[step], 1 - core).wait_recv()

    def r_first(n):
        for step in (1, 2, 0):
            r_start(step, n)

    for half in range(2):

        def norm_body(g, carry, half=half):
            group = half * 2 + (g // 2) * 4 + g % 2
            for pos in range(4):
                rows = pl.ds(group * 4 + pos, 64, stride=32)
                parts = center([x0[rows, :], x1[rows, :]], 256)
                for side in range(2):
                    lanes = slice(side * 128, side * 128 + 128)
                    high, low = split(parts[side] * gain[:, lanes] + offset[:, lanes])
                    at = pl.ds(pl.multiple_of(g * 64, 64), 64)
                    xh[half, at, pl.ds(pos * 256 + side * 128, 128)] = high
                    xl[half, at, pl.ds(pos * 256 + side * 128, 128)] = low
            return carry

        lax.fori_loop(0, 4, norm_body, 0)
        both = dot(xh[half], wh[...]) + dot(xl[half], wh[...]) + dot(xh[half], wl[...])
        for g in range(4):
            send_left[half + 2 * (g // 2), :, pl.ds((g % 2) * 128, 128)] = both[g * 64 : g * 64 + 64, :128]
        if half == 0:
            greeted = 7 + jnp.where(here_first, 0, 1) + jnp.where(here_second, 0, 1)
            pl.semaphore_wait(barrier, greeted)
        t_begin(half)
        t_begin(half + 2)
        for g in range(2):
            pair_rows = jnp.concatenate(
                [both[g * 64 : g * 64 + 64, 128:], both[g * 64 + 128 : g * 64 + 192, 128:]], axis=0
            )
            right[row, pl.ds((2 * half + g) * 128, 128), :] = pair_rows.T
            r_first(2 * half + g)

    for at in range(6, 9):
        loads[at].wait()

    def order_body(d, carry):
        high, low = split(pw[pl.ds(d, 32, stride=32), :])
        at = pl.ds(pl.multiple_of(d * 32, 32), 32)
        pwc[at, pl.ds(0, 128)] = high
        pwc[at, pl.ds(128, 128)] = low
        return carry

    lax.fori_loop(0, 32, order_body, 0)
    high, low = split(hw_ref[...])
    hwc[pl.ds(0, 128), :] = high
    hwc[pl.ds(128, 128), :] = high
    hwc[pl.ds(256, 128), :] = low
    high, low = split(fw_ref[...])
    fwc[:, pl.ds(0, 128)] = high
    fwc[:, pl.ds(128, 128)] = low

    def swap_first(n):
        t_pass(n)

    def swap_second(n):
        second_arrival(n).wait()
        for step in (1, 2, 0):
            l_start(step, n)
        c_start(0, n)

    def right_relay(step, further):
        def relay(n):
            r_wait(step, n)
            for later in further:
                r_start(later, n)

        return relay

    def left_relay(step, further):
        def relay(n):
            l_wait(step, n)
            for later in further:
                l_start(later, n)
            c_start(step + 1, n)

        return relay

    low_half = lax.broadcasted_iota(jnp.int32, (16, 128), 1) < 64

    def prepare(part):
        for n in range(CH):
            for step in ((), (3,), (2,), (5, 6))[part]:
                r_wait(step, n)
        p = (y + (0, 3, 1, 2)[part]) % 4

        def body(d, carry):
            a = right[2 * p, pl.ds(d, 16, stride=32), :]
            b = right[2 * p + 1, pl.ds(d, 16, stride=32), :]
            first = jnp.where(low_half, a, pltpu.roll(b, 64, 1))
            second = jnp.where(low_half, pltpu.roll(a, 64, 1), b)
            rows = pl.ds(pl.multiple_of(d * 32, 32), 32)
            high, low = split(jnp.concatenate([first, second], axis=0))
            lhs[rows, pl.ds(pl.multiple_of(p * 128, 128), 128)] = high
            lhs[rows, pl.ds(pl.multiple_of(512 + p * 128, 128), 128)] = low
            lhs[rows, pl.ds(pl.multiple_of(1024 + p * 128, 128), 128)] = high
            return carry

        lax.fori_loop(0, 32, body, 0, unroll=4)

    for at in range(9, 15):
        loads[at].wait()

    lane = lax.broadcasted_iota(jnp.int32, (32, 128), 1)
    below = lane < 64
    even = (lane // 32) % 2 == 0
    pbias, fbias, hbias = pbias_ref[...], fbias_ref[...], hbias_ref[...]
    pgain, poffset = pgain_ref[...], poffset_ref[...]

    def exchange_halves(a, b):
        moved = pltpu.roll(jnp.where(below, b, a), 64, 1)
        return jnp.where(below, a, moved), jnp.where(below, moved, b)

    def exchange_quarters(a, b):
        return jnp.where(even, a, pltpu.roll(b, 32, 1)), jnp.where(even, pltpu.roll(a, 96, 1), b)

    def outer(q):
        for h in range(2):
            high, low = split(left[q, h].reshape(512, 256))
            at = pl.ds(h * 256, 256)
            rhs[pl.ds(0, 512), at] = high
            rhs[pl.ds(512, 512), at] = high
            rhs[pl.ds(1024, 512), at] = low
        raw[q % 2] = dot(lhs[...], rhs[...])

    def finish(q):
        for t in range(8):
            for u in range(4):
                v = [raw[q % 2, pl.ds((4 * t + d) * 32, 32), pl.ds(u * 128, 128)] for d in range(4)]
                v[0], v[2] = exchange_halves(v[0], v[2])
                v[1], v[3] = exchange_halves(v[1], v[3])
                v[0], v[1] = exchange_quarters(v[0], v[1])
                v[2], v[3] = exchange_quarters(v[2], v[3])
                for i in range(4):
                    high, low = split(v[i])
                    oh[pl.ds((u * 4 + i) * 32, 32), pl.ds(t * 128, 128)] = high
                    ol[pl.ds((u * 4 + i) * 32, 32), pl.ds(t * 128, 128)] = low
        wide = dot(oh[...], pwc[...])
        update = wide[:, :128] + wide[:, 128:] + dot(ol[...], pwc[:, :128])
        tiles = [pl.ds((h * 32 + q * 8) * 32, 256) for h in range(2)]
        updated = jnp.concatenate([pair[rows, :] for rows in tiles], axis=0) + update * (1.0 / 512) + pbias
        (flat,) = center([updated], 128)
        high, low = split(flat * pgain + poffset)
        hidden = jnp.maximum(dot(jnp.concatenate([high, low, high], axis=1), hwc[...]) + hbias, 0.0)
        high, low = split(hidden)
        wide = dot(high, fwc[...])
        final = wide[:, :128] + wide[:, 128:] + dot(low, fwc[:, :128])
        result = updated + final + fbias
        for h in range(2):
            out[tiles[h], :] = result[h * 256 : h * 256 + 256]

    def store(q, h):
        rows = pl.ds(pl.multiple_of((h * 32 + q * 8) * 32, 256), 256)
        return pltpu.make_async_copy(out.at[rows, :], out_hbm.at[rows, :], out_sem.at[q * 2 + h])

    def arrive(q):
        for step in range(8):
            c_wait(step, q)

    def product(q):
        arrive(q)
        outer(q)

    def complete(q):
        finish(q)
        store(q, 0).start()
        store(q, 1).start()

    work = {
        "t1": swap_first,
        "t2": swap_second,
        "r0": right_relay(0, (3, 4)),
        "r1": right_relay(1, (5,)),
        "r4": right_relay(4, (6,)),
        "l0": left_relay(0, (3, 4)),
        "l1": left_relay(1, (5,)),
        "l2": left_relay(2, ()),
        "l3": left_relay(3, ()),
        "l4": left_relay(4, (6,)),
        "l5": left_relay(5, ()),
        "l6": left_relay(6, ()),
        "P": prepare,
        "O": product,
        "F": complete,
    }
    for name, n in ORDER:
        work[name](n)
    for n in range(CH):
        store(n, 0).wait()
        store(n, 1).wait()
    for n in range(CH):
        for step in range(7):
            r_copy(step, n, r_sent[step], r_to[step]).wait_send()
            l_copy(step, n, l_sent[step], l_to[step]).wait_send()
        for step in range(8):
            c_copy(step, n, c_slots[step], core).wait_send()

        @pl.when(jnp.logical_not(here_first))
        def _(n=n):
            first_copy(n).wait_send()

        @pl.when(jnp.logical_not(here_second))
        def _(n=n):
            second_copy(n).wait_send()


def on_device(
    alignment,
    align_gain,
    align_bias,
    left_weight,
    right_weight,
    project_weight,
    project_bias,
    pair_state,
    pair_gain,
    pair_bias,
    hidden_weight,
    hidden_bias,
    final_weight,
    final_bias,
):
    apart = pl.BlockSpec(memory_space=pl.ANY)
    dma = pltpu.SemaphoreType.DMA
    output = pl.pallas_call(
        kernel,
        out_shape=jax.ShapeDtypeStruct((2048, 128), F32),
        in_specs=[apart] * 14,
        out_specs=apart,
        scratch_shapes=[
            pltpu.VMEM((1, 256), F32),
            pltpu.VMEM((1, 256), F32),
            pltpu.VMEM((32, 256), F32),
            pltpu.VMEM((32, 256), F32),
            pltpu.VMEM((1, 128), F32),
            pltpu.VMEM((1, 128), F32),
            pltpu.VMEM((1, 128), F32),
            pltpu.VMEM((128, 512), F32),
            pltpu.VMEM((1, 512), F32),
            pltpu.VMEM((512, 128), F32),
            pltpu.VMEM((1, 128), F32),
            pltpu.VMEM((2048, 128), F32),
            pltpu.VMEM((2048, 128), F32),
            pltpu.VMEM((2, 256, 1024), BF16),
            pltpu.VMEM((2, 256, 1024), BF16),
            pltpu.VMEM((1024, 256), BF16),
            pltpu.VMEM((1024, 256), BF16),
            pltpu.VMEM((CH, 64, 256), F32),
            pltpu.VMEM((CH, 64, 256), F32),
            pltpu.VMEM((CH, 2, 8, 64, 256), F32),
            pltpu.VMEM((8, 512, 128), F32),
            pltpu.VMEM((1024, 1536), BF16),
            pltpu.VMEM((1536, 512), BF16),
            pltpu.VMEM((2, 1024, 512), F32),
            pltpu.VMEM((512, 1024), BF16),
            pltpu.VMEM((512, 1024), BF16),
            pltpu.VMEM((1024, 128), F32),
            pltpu.VMEM((1024, 256), BF16),
            pltpu.VMEM((384, 512), BF16),
            pltpu.VMEM((512, 256), BF16),
            pltpu.VMEM((2048, 128), F32),
            pltpu.VMEM((2048, 128), F32),
            dma((15,)),
            dma((7, CH)),
            dma((7, CH)),
            dma((7, CH)),
            dma((7, CH)),
            dma((8, CH)),
            dma((8, CH)),
            dma((2, CH)),
            dma((2, CH)),
            dma((8,)),
        ],
        compiler_params=pltpu.CompilerParams(
            collective_id=0, has_side_effects=True, vmem_limit_bytes=63 * 1024 * 1024
        ),
        cost_estimate=pl.CostEstimate(flops=10**10, bytes_accessed=6 * 10**6, transcendentals=0),
    )(
        alignment.reshape(2048, 256),
        align_gain.reshape(1, 256),
        align_bias.reshape(1, 256),
        left_weight.T,
        right_weight.T,
        project_weight,
        project_bias.reshape(1, 128),
        pair_state.reshape(2048, 128),
        pair_gain.reshape(1, 128),
        pair_bias.reshape(1, 128),
        hidden_weight,
        hidden_bias.reshape(1, 512),
        final_weight,
        final_bias.reshape(1, 128),
    )
    return output.reshape(64, 32, 128)


def solution(mesh):
    spread = P("row", "col", None)
    placed = (spread,) + (P(),) * 6 + (spread,) + (P(),) * 6
    return jax.shard_map(on_device, mesh=mesh, in_specs=placed, out_specs=spread, check_vma=False)
```

```python
import functools

import jax
import jax.numpy as jnp
from jax import lax
from jax.experimental import pallas as pl
from jax.experimental.pallas import tpu as pltpu
from jax.sharding import PartitionSpec as P

F32 = jnp.float32
BF16 = jnp.bfloat16
MESH = pl.DeviceIdType.MESH
CH = 4
ORDER = (
    ("r0", 0), ("t1", 0), ("t1", 2), ("t1", 1), ("t1", 3), ("r0", 2), ("r0", 3), ("r0", 1), ("r4", 0),
    ("r1", 3), ("P", 0), ("t2", 0), ("r1", 0), ("t2", 2), ("t2", 1), ("l1", 0), ("r1", 1), ("r4", 2),
    ("l2", 0), ("l0", 0), ("r4", 3), ("r1", 2), ("l1", 2), ("t2", 3), ("l2", 1), ("r4", 1), ("l1", 1),
    ("l5", 0), ("l0", 2), ("P", 1), ("l0", 1), ("l2", 2), ("l3", 0), ("P", 2), ("l4", 0), ("l5", 2),
    ("l0", 3), ("l5", 1), ("l2", 3), ("l6", 0), ("l1", 3), ("P", 3), ("l4", 2), ("O", 0), ("l6", 2),
    ("l3", 2), ("l3", 1), ("l4", 1), ("l4", 3), ("F", 0), ("l5", 3), ("O", 2), ("l3", 3), ("l6", 1), ("F", 2),
    ("l6", 3), ("O", 1), ("F", 1), ("O", 3), ("F", 3),
)


def split(value):
    high = value.astype(BF16)
    low = (value - high.astype(F32)).astype(BF16)
    return high, low


def dot(a, b):
    return jnp.dot(a, b, preferred_element_type=F32)


def center(values, width):
    total = values[0]
    for part in values[1:]:
        total = total + part
    middle = jnp.sum(total, axis=-1, keepdims=True) * (1.0 / width)
    values = [part - middle for part in values]
    total = values[0] * values[0]
    for part in values[1:]:
        total = total + part * part
    spread = jnp.sum(total, axis=-1, keepdims=True) * (1.0 / width)
    factor = lax.rsqrt(spread + 1e-05)
    return [part * factor for part in values]


def kernel(
    align,
    gain_hbm,
    offset_hbm,
    lw_hbm,
    rw_hbm,
    pw_hbm,
    pbias_hbm,
    pair_hbm,
    pgain_hbm,
    poffset_hbm,
    hw_hbm,
    hbias_hbm,
    fw_hbm,
    fbias_hbm,
    out_hbm,
    gain_ref,
    offset_ref,
    lw_ref,
    rw_ref,
    pbias_ref,
    pgain_ref,
    poffset_ref,
    hw_ref,
    hbias_ref,
    fw_ref,
    fbias_ref,
    x0,
    x1,
    xh,
    xl,
    wh,
    wl,
    send_left,
    passing,
    left,
    right,
    lhs,
    rhs,
    raw,
    oh,
    ol,
    pw,
    pwc,
    hwc,
    fwc,
    pair,
    out,
    load_sem,
    r_send,
    r_recv,
    l_send,
    l_recv,
    c_send,
    c_recv,
    t_send,
    t_recv,
    out_sem,
):
    row, col = lax.axis_index("row"), lax.axis_index("col")
    y, x_hi = row // 2, row % 2
    k, core = col // 2, col % 2
    x_lo, z = k // 4, k % 4

    def at_row(y_, x_):
        return (y_ % 4) * 2 + x_

    def at_k(x_, z_):
        return x_ * 4 + z_ % 4

    def same_col(r):
        return (r, col)

    def same_row(k_):
        return (row, k_ * 2 + core)

    other_core = (row, k * 2 + 1 - core)
    t_y = 2 * x_lo + z // 2
    t_x = jnp.where(x_hi == z % 2, x_lo, 1 - x_lo)
    t_z = (z + y - t_y + 4) % 4
    first_to = (y * 2 + z % 2, (t_x * 4 + t_z) * 2 + core)
    mid = (z - y - x_hi + 8) % 4
    mid_x, mid_w = mid // 2, mid % 2
    mid_hi = jnp.where(x_lo == mid_x, x_hi, 1 - x_hi)
    first_from = (y * 2 + mid_hi, (mid_x * 4 + 2 * mid_w + x_hi) * 2 + core)
    mid_shard = y * 2 + mid_hi
    mid_y = 2 * mid_x + mid_w
    second_to = (mid_y * 2 + x_hi, col)

    def shard_at(x_, z_):
        return ((z_ - y % 2 - x_hi + 2 * (y // 2) + 8) % 4) * 2 + jnp.where(x_ == y // 2, x_hi, 1 - x_hi)

    shard = shard_at(x_lo, z)
    second_from = ((shard // 2) * 2 + x_hi, col)
    here_first = jnp.logical_and(first_to[0] == row, first_to[1] == col)
    here_second = mid_y == y
    y_up, y_down = same_col(at_row(y + 1, x_hi)), same_col(at_row(y + 3, x_hi))
    x_far = same_col(at_row(y, 1 - x_hi))
    z_up, z_down = same_row(at_k(x_lo, z + 1)), same_row(at_k(x_lo, z + 3))
    x_near = same_row(at_k(1 - x_lo, z))

    moves = [
        (lw_hbm, lw_ref),
        (rw_hbm, rw_ref),
        (align.at[:, pl.ds(0, 128)], x0),
        (align.at[:, pl.ds(128, 128)], x1),
        (gain_hbm, gain_ref),
        (offset_hbm, offset_ref),
        (pw_hbm, pw),
        (hw_hbm, hw_ref),
        (fw_hbm, fw_ref),
        (pair_hbm, pair),
        (pbias_hbm, pbias_ref),
        (pgain_hbm, pgain_ref),
        (poffset_hbm, poffset_ref),
        (hbias_hbm, hbias_ref),
        (fbias_hbm, fbias_ref),
    ]
    loads = [pltpu.make_async_copy(source, target, load_sem.at[at]) for at, (source, target) in enumerate(moves)]
    for load in loads:
        load.start()

    barrier = pltpu.get_barrier_semaphore()
    for device in (other_core, y_up, y_down, x_far, z_up, z_down, x_near):
        pl.semaphore_signal(barrier, inc=1, device_id=device, device_id_type=MESH)

    for device in (first_from, second_from):

        @pl.when(jnp.logical_or(device[0] != row, device[1] != col))
        def _(device=device):
            pl.semaphore_signal(barrier, inc=1, device_id=device, device_id_type=MESH)

    lane = lax.broadcasted_iota(jnp.int32, (256, 128), 1)
    loads[0].wait()
    loads[1].wait()
    for source, at in ((lw_ref, 0), (rw_ref, 128)):
        wide = jnp.concatenate([source[...]] * 4, axis=0).T
        for pos in range(4):
            placed = jnp.where(lane // 32 == pos, wide, 0.0)
            high, low = split(placed)
            wh[pl.ds(pos * 256, 256), pl.ds(at, 128)] = high
            wl[pl.ds(pos * 256, 256), pl.ds(at, 128)] = low

    for at in range(2, 6):
        loads[at].wait()

    gain = gain_ref[...]
    offset = offset_ref[...]

    def r_copy(step, n, slot, device):
        block = right.at[slot, pl.ds(n * 128, 128), :]
        return pltpu.make_async_remote_copy(
            src_ref=block,
            dst_ref=block,
            send_sem=r_send.at[step, n],
            recv_sem=r_recv.at[step, n],
            device_id=device,
            device_id_type=MESH,
        )

    def l_copy(step, n, slot, device):
        block = left.at[n, core, slot]
        return pltpu.make_async_remote_copy(
            src_ref=block,
            dst_ref=block,
            send_sem=l_send.at[step, n],
            recv_sem=l_recv.at[step, n],
            device_id=device,
            device_id_type=MESH,
        )

    def c_copy(step, n, slot, half):
        block = left.at[n, half, slot]
        return pltpu.make_async_remote_copy(
            src_ref=block,
            dst_ref=block,
            send_sem=c_send.at[step, n],
            recv_sem=c_recv.at[step, n],
            device_id=other_core,
            device_id_type=MESH,
        )

    def first_copy(n):
        return pltpu.make_async_remote_copy(
            src_ref=send_left.at[n],
            dst_ref=passing.at[n],
            send_sem=t_send.at[0, n],
            recv_sem=t_recv.at[0, n],
            device_id=first_to,
            device_id_type=MESH,
        )

    def second_copy(n):
        return pltpu.make_async_remote_copy(
            src_ref=passing.at[n],
            dst_ref=left.at[n, core, mid_shard],
            send_sem=t_send.at[1, n],
            recv_sem=t_recv.at[1, n],
            device_id=second_to,
            device_id_type=MESH,
        )

    def first_arrival(n):
        return pltpu.make_async_copy(send_left.at[n], passing.at[n], t_recv.at[0, n])

    def second_arrival(n):
        return pltpu.make_async_copy(passing.at[n], left.at[n, core, shard], t_recv.at[1, n])

    def t_begin(n):
        @pl.when(jnp.logical_not(here_first))
        def _():
            first_copy(n).start()

        @pl.when(here_first)
        def _():
            first_arrival(n).start()

    def t_pass(n):
        first_arrival(n).wait()

        @pl.when(jnp.logical_not(here_second))
        def _():
            second_copy(n).start()

        @pl.when(here_second)
        def _():
            second_arrival(n).start()

    r_sent = [row, row, row, at_row(y, 1 - x_hi), at_row(y, 1 - x_hi), at_row(y + 3, x_hi), at_row(y + 1, 1 - x_hi)]
    r_to = [x_far, y_up, y_down, y_up, y_down, y_up, y_down]
    r_lands = [
        at_row(y, 1 - x_hi),
        at_row(y + 3, x_hi),
        at_row(y + 1, x_hi),
        at_row(y + 3, 1 - x_hi),
        at_row(y + 1, 1 - x_hi),
        at_row(y + 2, x_hi),
        at_row(y + 2, 1 - x_hi),
    ]
    x_other = 1 - x_lo
    l_sent = [
        shard,
        shard,
        shard,
        shard_at(x_other, z),
        shard_at(x_other, z),
        None,
        shard_at(x_lo, z + 2),
    ]
    l_to = [x_near, z_up, z_down, z_up, z_down, None, x_near]
    far_sent = (shard_at(x_lo, z + 3), shard_at(x_lo, z + 1))
    far_to = (z_up, z_down)
    l_lands = [
        shard_at(x_other, z),
        shard_at(x_lo, z + 3),
        shard_at(x_lo, z + 1),
        shard_at(x_other, z + 3),
        shard_at(x_other, z + 1),
        shard_at(x_lo, z + 2),
        shard_at(x_other, z + 2),
    ]
    c_slots = [shard] + l_lands

    def r_start(step, n):
        r_copy(step, n, r_sent[step], r_to[step]).start()

    def r_wait(step, n):
        r_copy(step, n, r_lands[step], r_to[step]).wait_recv()

    def l_sends(step, n):
        if step == 5:
            return l_copy(step, n, far_sent[n % 2], far_to[n % 2])
        return l_copy(step, n, l_sent[step], l_to[step])

    def l_start(step, n):
        l_sends(step, n).start()

    def l_wait(step, n):
        l_copy(step, n, l_lands[step], x_near).wait_recv()

    def c_start(step, n):
        c_copy(step, n, c_slots[step], core).start()

    def c_wait(step, n):
        c_copy(step, n, c_slots[step], 1 - core).wait_recv()

    def r_first(n):
        for step in (1, 2, 0):
            r_start(step, n)

    for half in range(2):

        def norm_body(g, carry, half=half):
            group = half * 2 + (g // 2) * 4 + g % 2
            for pos in range(4):
                rows = pl.ds(group * 4 + pos, 64, stride=32)
                parts = center([x0[rows, :], x1[rows, :]], 256)
                for side in range(2):
                    lanes = slice(side * 128, side * 128 + 128)
                    high, low = split(parts[side] * gain[:, lanes] + offset[:, lanes])
                    at = pl.ds(pl.multiple_of(g * 64, 64), 64)
                    xh[half, at, pl.ds(pos * 256 + side * 128, 128)] = high
                    xl[half, at, pl.ds(pos * 256 + side * 128, 128)] = low
            return carry

        lax.fori_loop(0, 4, norm_body, 0)
        both = dot(xh[half], wh[...]) + dot(xl[half], wh[...]) + dot(xh[half], wl[...])
        for g in range(4):
            send_left[half + 2 * (g // 2), :, pl.ds((g % 2) * 128, 128)] = both[g * 64 : g * 64 + 64, :128]
        if half == 0:
            greeted = 7 + jnp.where(here_first, 0, 1) + jnp.where(here_second, 0, 1)
            pl.semaphore_wait(barrier, greeted)
        t_begin(half)
        t_begin(half + 2)
        for g in range(2):
            pair_rows = jnp.concatenate(
                [both[g * 64 : g * 64 + 64, 128:], both[g * 64 + 128 : g * 64 + 192, 128:]], axis=0
            )
            right[row, pl.ds((2 * half + g) * 128, 128), :] = pair_rows.T
            r_first(2 * half + g)

    for at in range(6, 9):
        loads[at].wait()

    def order_body(d, carry):
        high, low = split(pw[pl.ds(d, 32, stride=32), :])
        at = pl.ds(pl.multiple_of(d * 32, 32), 32)
        pwc[at, pl.ds(0, 128)] = high
        pwc[at, pl.ds(128, 128)] = low
        return carry

    lax.fori_loop(0, 32, order_body, 0)
    high, low = split(hw_ref[...])
    hwc[pl.ds(0, 128), :] = high
    hwc[pl.ds(128, 128), :] = high
    hwc[pl.ds(256, 128), :] = low
    high, low = split(fw_ref[...])
    fwc[:, pl.ds(0, 128)] = high
    fwc[:, pl.ds(128, 128)] = low

    def swap_first(n):
        t_pass(n)

    def swap_second(n):
        second_arrival(n).wait()
        for step in (1, 2, 0):
            l_start(step, n)
        c_start(0, n)

    def right_relay(step, further):
        def relay(n):
            r_wait(step, n)
            for later in further:
                r_start(later, n)

        return relay

    def left_relay(step, further):
        def relay(n):
            l_wait(step, n)
            for later in further:
                l_start(later, n)
            if step == 1 + n % 2:
                l_start(5, n)
            c_start(step + 1, n)

        return relay

    low_half = lax.broadcasted_iota(jnp.int32, (16, 128), 1) < 64

    def prepare(part):
        for n in range(CH):
            for step in ((), (3,), (2,), (5, 6))[part]:
                r_wait(step, n)
        p = (y + (0, 3, 1, 2)[part]) % 4

        def body(d, carry):
            a = right[2 * p, pl.ds(d, 16, stride=32), :]
            b = right[2 * p + 1, pl.ds(d, 16, stride=32), :]
            first = jnp.where(low_half, a, pltpu.roll(b, 64, 1))
            second = jnp.where(low_half, pltpu.roll(a, 64, 1), b)
            rows = pl.ds(pl.multiple_of(d * 32, 32), 32)
            high, low = split(jnp.concatenate([first, second], axis=0))
            lhs[rows, pl.ds(pl.multiple_of(p * 128, 128), 128)] = high
            lhs[rows, pl.ds(pl.multiple_of(512 + p * 128, 128), 128)] = low
            lhs[rows, pl.ds(pl.multiple_of(1024 + p * 128, 128), 128)] = high
            return carry

        lax.fori_loop(0, 32, body, 0, unroll=4)

    for at in range(9, 15):
        loads[at].wait()

    lane = lax.broadcasted_iota(jnp.int32, (32, 128), 1)
    below = lane < 64
    even = (lane // 32) % 2 == 0
    pbias, fbias, hbias = pbias_ref[...], fbias_ref[...], hbias_ref[...]
    pgain, poffset = pgain_ref[...], poffset_ref[...]

    def exchange_halves(a, b):
        moved = pltpu.roll(jnp.where(below, b, a), 64, 1)
        return jnp.where(below, a, moved), jnp.where(below, moved, b)

    def exchange_quarters(a, b):
        return jnp.where(even, a, pltpu.roll(b, 32, 1)), jnp.where(even, pltpu.roll(a, 96, 1), b)

    def outer(q):
        for h in range(2):
            high, low = split(left[q, h].reshape(512, 256))
            at = pl.ds(h * 256, 256)
            rhs[pl.ds(0, 512), at] = high
            rhs[pl.ds(512, 512), at] = high
            rhs[pl.ds(1024, 512), at] = low
        raw[q % 2] = dot(lhs[...], rhs[...])

    def finish(q):
        for t in range(8):
            for u in range(4):
                v = [raw[q % 2, pl.ds((4 * t + d) * 32, 32), pl.ds(u * 128, 128)] for d in range(4)]
                v[0], v[2] = exchange_halves(v[0], v[2])
                v[1], v[3] = exchange_halves(v[1], v[3])
                v[0], v[1] = exchange_quarters(v[0], v[1])
                v[2], v[3] = exchange_quarters(v[2], v[3])
                for i in range(4):
                    high, low = split(v[i])
                    oh[pl.ds((u * 4 + i) * 32, 32), pl.ds(t * 128, 128)] = high
                    ol[pl.ds((u * 4 + i) * 32, 32), pl.ds(t * 128, 128)] = low
        wide = dot(oh[...], pwc[...])
        update = wide[:, :128] + wide[:, 128:] + dot(ol[...], pwc[:, :128])
        tiles = [pl.ds((h * 32 + q * 8) * 32, 256) for h in range(2)]
        updated = jnp.concatenate([pair[rows, :] for rows in tiles], axis=0) + update * (1.0 / 512) + pbias
        (flat,) = center([updated], 128)
        high, low = split(flat * pgain + poffset)
        hidden = jnp.maximum(dot(jnp.concatenate([high, low, high], axis=1), hwc[...]) + hbias, 0.0)
        high, low = split(hidden)
        wide = dot(high, fwc[...])
        final = wide[:, :128] + wide[:, 128:] + dot(low, fwc[:, :128])
        result = updated + final + fbias
        for h in range(2):
            out[tiles[h], :] = result[h * 256 : h * 256 + 256]

    def store(q, h):
        rows = pl.ds(pl.multiple_of((h * 32 + q * 8) * 32, 256), 256)
        return pltpu.make_async_copy(out.at[rows, :], out_hbm.at[rows, :], out_sem.at[q * 2 + h])

    def arrive(q):
        for step in range(8):
            c_wait(step, q)

    def product(q):
        arrive(q)
        outer(q)

    def complete(q):
        finish(q)
        store(q, 0).start()
        store(q, 1).start()

    work = {
        "t1": swap_first,
        "t2": swap_second,
        "r0": right_relay(0, (3, 4)),
        "r1": right_relay(1, (5,)),
        "r4": right_relay(4, (6,)),
        "l0": left_relay(0, (3, 4)),
        "l1": left_relay(1, ()),
        "l2": left_relay(2, ()),
        "l3": left_relay(3, ()),
        "l4": left_relay(4, ()),
        "l5": left_relay(5, (6,)),
        "l6": left_relay(6, ()),
        "P": prepare,
        "O": product,
        "F": complete,
    }
    for name, n in ORDER:
        work[name](n)
    for n in range(CH):
        store(n, 0).wait()
        store(n, 1).wait()
    for n in range(CH):
        for step in range(7):
            r_copy(step, n, r_sent[step], r_to[step]).wait_send()
            l_sends(step, n).wait_send()
        for step in range(8):
            c_copy(step, n, c_slots[step], core).wait_send()

        @pl.when(jnp.logical_not(here_first))
        def _(n=n):
            first_copy(n).wait_send()

        @pl.when(jnp.logical_not(here_second))
        def _(n=n):
            second_copy(n).wait_send()


def on_device(
    alignment,
    align_gain,
    align_bias,
    left_weight,
    right_weight,
    project_weight,
    project_bias,
    pair_state,
    pair_gain,
    pair_bias,
    hidden_weight,
    hidden_bias,
    final_weight,
    final_bias,
):
    apart = pl.BlockSpec(memory_space=pl.ANY)
    dma = pltpu.SemaphoreType.DMA
    output = pl.pallas_call(
        kernel,
        out_shape=jax.ShapeDtypeStruct((2048, 128), F32),
        in_specs=[apart] * 14,
        out_specs=apart,
        scratch_shapes=[
            pltpu.VMEM((1, 256), F32),
            pltpu.VMEM((1, 256), F32),
            pltpu.VMEM((32, 256), F32),
            pltpu.VMEM((32, 256), F32),
            pltpu.VMEM((1, 128), F32),
            pltpu.VMEM((1, 128), F32),
            pltpu.VMEM((1, 128), F32),
            pltpu.VMEM((128, 512), F32),
            pltpu.VMEM((1, 512), F32),
            pltpu.VMEM((512, 128), F32),
            pltpu.VMEM((1, 128), F32),
            pltpu.VMEM((2048, 128), F32),
            pltpu.VMEM((2048, 128), F32),
            pltpu.VMEM((2, 256, 1024), BF16),
            pltpu.VMEM((2, 256, 1024), BF16),
            pltpu.VMEM((1024, 256), BF16),
            pltpu.VMEM((1024, 256), BF16),
            pltpu.VMEM((CH, 64, 256), F32),
            pltpu.VMEM((CH, 64, 256), F32),
            pltpu.VMEM((CH, 2, 8, 64, 256), F32),
            pltpu.VMEM((8, 512, 128), F32),
            pltpu.VMEM((1024, 1536), BF16),
            pltpu.VMEM((1536, 512), BF16),
            pltpu.VMEM((2, 1024, 512), F32),
            pltpu.VMEM((512, 1024), BF16),
            pltpu.VMEM((512, 1024), BF16),
            pltpu.VMEM((1024, 128), F32),
            pltpu.VMEM((1024, 256), BF16),
            pltpu.VMEM((384, 512), BF16),
            pltpu.VMEM((512, 256), BF16),
            pltpu.VMEM((2048, 128), F32),
            pltpu.VMEM((2048, 128), F32),
            dma((15,)),
            dma((7, CH)),
            dma((7, CH)),
            dma((7, CH)),
            dma((7, CH)),
            dma((8, CH)),
            dma((8, CH)),
            dma((2, CH)),
            dma((2, CH)),
            dma((8,)),
        ],
        compiler_params=pltpu.CompilerParams(
            collective_id=0, has_side_effects=True, vmem_limit_bytes=63 * 1024 * 1024
        ),
        cost_estimate=pl.CostEstimate(flops=10**10, bytes_accessed=6 * 10**6, transcendentals=0),
    )(
        alignment.reshape(2048, 256),
        align_gain.reshape(1, 256),
        align_bias.reshape(1, 256),
        left_weight.T,
        right_weight.T,
        project_weight,
        project_bias.reshape(1, 128),
        pair_state.reshape(2048, 128),
        pair_gain.reshape(1, 128),
        pair_bias.reshape(1, 128),
        hidden_weight,
        hidden_bias.reshape(1, 512),
        final_weight,
        final_bias.reshape(1, 128),
    )
    return output.reshape(64, 32, 128)


def solution(mesh):
    spread = P("row", "col", None)
    placed = (spread,) + (P(),) * 6 + (spread,) + (P(),) * 6
    return jax.shard_map(on_device, mesh=mesh, in_specs=placed, out_specs=spread, check_vma=False)
```

```python
import functools

import jax
import jax.numpy as jnp
from jax import lax
from jax.experimental import pallas as pl
from jax.experimental.pallas import tpu as pltpu
from jax.sharding import PartitionSpec as P

F32 = jnp.float32
BF16 = jnp.bfloat16
MESH = pl.DeviceIdType.MESH
CH = 4
ORDER = (
    ("r0", 0), ("t1", 0), ("t1", 2), ("t1", 1), ("t1", 3), ("r0", 2), ("r0", 3), ("r0", 1), ("r4", 0),
    ("r1", 3), ("P", 0), ("t2", 0), ("r1", 0), ("t2", 2), ("t2", 1), ("l1", 0), ("r1", 1), ("r4", 2),
    ("l2", 0), ("l0", 0), ("r4", 3), ("r1", 2), ("l1", 2), ("t2", 3), ("l2", 1), ("r4", 1), ("l1", 1),
    ("l5", 0), ("l0", 2), ("P", 1), ("l0", 1), ("l2", 2), ("l3", 0), ("P", 2), ("l4", 0), ("l5", 2),
    ("l0", 3), ("l5", 1), ("l2", 3), ("l6", 0), ("l1", 3), ("P", 3), ("l4", 2), ("O", 0), ("l6", 2),
    ("l3", 2), ("l3", 1), ("l4", 1), ("l4", 3), ("F", 0), ("l5", 3), ("O", 2), ("l3", 3), ("l6", 1), ("F", 2),
    ("l6", 3), ("O", 1), ("F", 1), ("O", 3), ("F", 3),
)


def split(value):
    high = value.astype(BF16)
    low = (value - high.astype(F32)).astype(BF16)
    return high, low


def dot(a, b):
    return jnp.dot(a, b, preferred_element_type=F32)


def center(values, width):
    total = values[0]
    for part in values[1:]:
        total = total + part
    middle = jnp.sum(total, axis=-1, keepdims=True) * (1.0 / width)
    values = [part - middle for part in values]
    total = values[0] * values[0]
    for part in values[1:]:
        total = total + part * part
    spread = jnp.sum(total, axis=-1, keepdims=True) * (1.0 / width)
    factor = lax.rsqrt(spread + 1e-05)
    return [part * factor for part in values]


def kernel(
    align,
    gain_hbm,
    offset_hbm,
    lw_hbm,
    rw_hbm,
    pw_hbm,
    pbias_hbm,
    pair_hbm,
    pgain_hbm,
    poffset_hbm,
    hw_hbm,
    hbias_hbm,
    fw_hbm,
    fbias_hbm,
    out_hbm,
    gain_ref,
    offset_ref,
    lw_ref,
    rw_ref,
    pbias_ref,
    pgain_ref,
    poffset_ref,
    hw_ref,
    hbias_ref,
    fw_ref,
    fbias_ref,
    x0,
    x1,
    xh,
    xl,
    wh,
    wl,
    send_left,
    passing,
    left,
    right,
    lhs,
    rhs,
    raw,
    oh,
    ol,
    pw,
    pwc,
    hwc,
    fwc,
    pair,
    out,
    load_sem,
    r_send,
    r_recv,
    l_send,
    l_recv,
    c_send,
    c_recv,
    t_send,
    t_recv,
    out_sem,
):
    row, col = lax.axis_index("row"), lax.axis_index("col")
    y, x_hi = row // 2, row % 2
    k, core = col // 2, col % 2
    x_lo, z = k // 4, k % 4

    def at_row(y_, x_):
        return (y_ % 4) * 2 + x_

    def at_k(x_, z_):
        return x_ * 4 + z_ % 4

    def same_col(r):
        return (r, col)

    def same_row(k_):
        return (row, k_ * 2 + core)

    other_core = (row, k * 2 + 1 - core)
    t_y = 2 * x_lo + z // 2
    t_x = jnp.where(x_hi == z % 2, x_lo, 1 - x_lo)
    t_z = (z + y - t_y + 4) % 4
    first_to = (y * 2 + z % 2, (t_x * 4 + t_z) * 2 + core)
    mid = (z - y - x_hi + 8) % 4
    mid_x, mid_w = mid // 2, mid % 2
    mid_hi = jnp.where(x_lo == mid_x, x_hi, 1 - x_hi)
    first_from = (y * 2 + mid_hi, (mid_x * 4 + 2 * mid_w + x_hi) * 2 + core)
    mid_shard = y * 2 + mid_hi
    mid_y = 2 * mid_x + mid_w
    second_to = (mid_y * 2 + x_hi, col)

    def shard_at(x_, z_):
        return ((z_ - y % 2 - x_hi + 2 * (y // 2) + 8) % 4) * 2 + jnp.where(x_ == y // 2, x_hi, 1 - x_hi)

    shard = shard_at(x_lo, z)
    second_from = ((shard // 2) * 2 + x_hi, col)
    here_first = jnp.logical_and(first_to[0] == row, first_to[1] == col)
    here_second = mid_y == y
    y_up, y_down = same_col(at_row(y + 1, x_hi)), same_col(at_row(y + 3, x_hi))
    x_far = same_col(at_row(y, 1 - x_hi))
    z_up, z_down = same_row(at_k(x_lo, z + 1)), same_row(at_k(x_lo, z + 3))
    x_near = same_row(at_k(1 - x_lo, z))

    barrier = pltpu.get_barrier_semaphore()
    for device in (other_core, y_up, y_down, x_far, z_up, z_down, x_near):
        pl.semaphore_signal(barrier, inc=1, device_id=device, device_id_type=MESH)

    for device in (first_from, second_from):

        @pl.when(jnp.logical_or(device[0] != row, device[1] != col))
        def _(device=device):
            pl.semaphore_signal(barrier, inc=1, device_id=device, device_id_type=MESH)

    moves = [
        (lw_hbm, lw_ref),
        (rw_hbm, rw_ref),
        (align.at[:, pl.ds(0, 128)], x0),
        (align.at[:, pl.ds(128, 128)], x1),
        (gain_hbm, gain_ref),
        (offset_hbm, offset_ref),
        (pw_hbm, pw),
        (hw_hbm, hw_ref),
        (fw_hbm, fw_ref),
        (pair_hbm, pair),
        (pbias_hbm, pbias_ref),
        (pgain_hbm, pgain_ref),
        (poffset_hbm, poffset_ref),
        (hbias_hbm, hbias_ref),
        (fbias_hbm, fbias_ref),
    ]
    loads = [pltpu.make_async_copy(source, target, load_sem.at[at]) for at, (source, target) in enumerate(moves)]
    for at in (2, 3, 0, 1, *range(4, 15)):
        loads[at].start()

    lane = lax.broadcasted_iota(jnp.int32, (256, 128), 1)
    loads[0].wait()
    loads[1].wait()
    for source, at in ((lw_ref, 0), (rw_ref, 128)):
        wide = jnp.concatenate([source[...]] * 4, axis=0).T
        for pos in range(4):
            placed = jnp.where(lane // 32 == pos, wide, 0.0)
            high, low = split(placed)
            wh[pl.ds(pos * 256, 256), pl.ds(at, 128)] = high
            wl[pl.ds(pos * 256, 256), pl.ds(at, 128)] = low

    for at in range(2, 6):
        loads[at].wait()

    gain = gain_ref[...]
    offset = offset_ref[...]

    def r_copy(step, n, slot, device):
        block = right.at[slot, pl.ds(n * 128, 128), :]
        return pltpu.make_async_remote_copy(
            src_ref=block,
            dst_ref=block,
            send_sem=r_send.at[step, n],
            recv_sem=r_recv.at[step, n],
            device_id=device,
            device_id_type=MESH,
        )

    def l_copy(step, n, slot, device):
        block = left.at[n, core, slot]
        return pltpu.make_async_remote_copy(
            src_ref=block,
            dst_ref=block,
            send_sem=l_send.at[step, n],
            recv_sem=l_recv.at[step, n],
            device_id=device,
            device_id_type=MESH,
        )

    def c_copy(step, n, slot, half):
        block = left.at[n, half, slot]
        return pltpu.make_async_remote_copy(
            src_ref=block,
            dst_ref=block,
            send_sem=c_send.at[step, n],
            recv_sem=c_recv.at[step, n],
            device_id=other_core,
            device_id_type=MESH,
        )

    def first_copy(n):
        return pltpu.make_async_remote_copy(
            src_ref=send_left.at[n],
            dst_ref=passing.at[n],
            send_sem=t_send.at[0, n],
            recv_sem=t_recv.at[0, n],
            device_id=first_to,
            device_id_type=MESH,
        )

    def second_copy(n):
        return pltpu.make_async_remote_copy(
            src_ref=passing.at[n],
            dst_ref=left.at[n, core, mid_shard],
            send_sem=t_send.at[1, n],
            recv_sem=t_recv.at[1, n],
            device_id=second_to,
            device_id_type=MESH,
        )

    def first_arrival(n):
        return pltpu.make_async_copy(send_left.at[n], passing.at[n], t_recv.at[0, n])

    def second_arrival(n):
        return pltpu.make_async_copy(passing.at[n], left.at[n, core, shard], t_recv.at[1, n])

    def t_begin(n):
        @pl.when(jnp.logical_not(here_first))
        def _():
            first_copy(n).start()

        @pl.when(here_first)
        def _():
            first_arrival(n).start()

    def t_pass(n):
        first_arrival(n).wait()

        @pl.when(jnp.logical_not(here_second))
        def _():
            second_copy(n).start()

        @pl.when(here_second)
        def _():
            second_arrival(n).start()

    r_sent = [row, row, row, at_row(y, 1 - x_hi), at_row(y, 1 - x_hi), at_row(y + 3, x_hi), at_row(y + 1, 1 - x_hi)]
    r_to = [x_far, y_up, y_down, y_up, y_down, y_up, y_down]
    r_lands = [
        at_row(y, 1 - x_hi),
        at_row(y + 3, x_hi),
        at_row(y + 1, x_hi),
        at_row(y + 3, 1 - x_hi),
        at_row(y + 1, 1 - x_hi),
        at_row(y + 2, x_hi),
        at_row(y + 2, 1 - x_hi),
    ]
    x_other = 1 - x_lo
    l_sent = [
        shard,
        shard,
        shard,
        shard_at(x_other, z),
        shard_at(x_other, z),
        None,
        shard_at(x_lo, z + 2),
    ]
    l_to = [x_near, z_up, z_down, z_up, z_down, None, x_near]
    far_sent = (shard_at(x_lo, z + 3), shard_at(x_lo, z + 1))
    far_to = (z_up, z_down)
    l_lands = [
        shard_at(x_other, z),
        shard_at(x_lo, z + 3),
        shard_at(x_lo, z + 1),
        shard_at(x_other, z + 3),
        shard_at(x_other, z + 1),
        shard_at(x_lo, z + 2),
        shard_at(x_other, z + 2),
    ]
    c_slots = [shard] + l_lands

    def r_start(step, n):
        r_copy(step, n, r_sent[step], r_to[step]).start()

    def r_wait(step, n):
        r_copy(step, n, r_lands[step], r_to[step]).wait_recv()

    def l_sends(step, n):
        if step == 5:
            return l_copy(step, n, far_sent[n % 2], far_to[n % 2])
        return l_copy(step, n, l_sent[step], l_to[step])

    def l_start(step, n):
        l_sends(step, n).start()

    def l_wait(step, n):
        l_copy(step, n, l_lands[step], x_near).wait_recv()

    def c_start(step, n):
        c_copy(step, n, c_slots[step], core).start()

    def c_wait(step, n):
        c_copy(step, n, c_slots[step], 1 - core).wait_recv()

    def r_first(n):
        for step in (1, 2, 0):
            r_start(step, n)

    for half in range(2):

        def norm_body(g, carry, half=half):
            group = half * 2 + (g // 2) * 4 + g % 2
            for pos in range(4):
                rows = pl.ds(group * 4 + pos, 64, stride=32)
                parts = center([x0[rows, :], x1[rows, :]], 256)
                for side in range(2):
                    lanes = slice(side * 128, side * 128 + 128)
                    high, low = split(parts[side] * gain[:, lanes] + offset[:, lanes])
                    at = pl.ds(pl.multiple_of(g * 64, 64), 64)
                    xh[half, at, pl.ds(pos * 256 + side * 128, 128)] = high
                    xl[half, at, pl.ds(pos * 256 + side * 128, 128)] = low
            return carry

        lax.fori_loop(0, 4, norm_body, 0, unroll=2)
        both = dot(xh[half], wh[...]) + dot(xl[half], wh[...]) + dot(xh[half], wl[...])
        for g in range(4):
            send_left[half + 2 * (g // 2), :, pl.ds((g % 2) * 128, 128)] = both[g * 64 : g * 64 + 64, :128]
        if half == 0:
            greeted = 7 + jnp.where(here_first, 0, 1) + jnp.where(here_second, 0, 1)
            pl.semaphore_wait(barrier, greeted)
        t_begin(half)
        t_begin(half + 2)
        for g in range(2):
            pair_rows = jnp.concatenate(
                [both[g * 64 : g * 64 + 64, 128:], both[g * 64 + 128 : g * 64 + 192, 128:]], axis=0
            )
            right[row, pl.ds((2 * half + g) * 128, 128), :] = pair_rows.T
            r_first(2 * half + g)

    for at in range(6, 9):
        loads[at].wait()

    def order_body(d, carry):
        high, low = split(pw[pl.ds(d, 32, stride=32), :])
        at = pl.ds(pl.multiple_of(d * 32, 32), 32)
        pwc[at, pl.ds(0, 128)] = high
        pwc[at, pl.ds(128, 128)] = low
        return carry

    lax.fori_loop(0, 32, order_body, 0)
    high, low = split(hw_ref[...])
    hwc[pl.ds(0, 128), :] = high
    hwc[pl.ds(128, 128), :] = high
    hwc[pl.ds(256, 128), :] = low
    high, low = split(fw_ref[...])
    fwc[:, pl.ds(0, 128)] = high
    fwc[:, pl.ds(128, 128)] = low

    def swap_first(n):
        t_pass(n)

    def swap_second(n):
        second_arrival(n).wait()
        for step in (1, 2, 0):
            l_start(step, n)
        c_start(0, n)

    def right_relay(step, further):
        def relay(n):
            r_wait(step, n)
            for later in further:
                r_start(later, n)

        return relay

    def left_relay(step, further):
        def relay(n):
            l_wait(step, n)
            for later in further:
                l_start(later, n)
            if step == 1 + n % 2:
                l_start(5, n)
            c_start(step + 1, n)

        return relay

    low_half = lax.broadcasted_iota(jnp.int32, (16, 128), 1) < 64

    def prepare(part):
        for n in range(CH):
            for step in ((), (3,), (2,), (5, 6))[part]:
                r_wait(step, n)
        p = (y + (0, 3, 1, 2)[part]) % 4

        def body(d, carry):
            a = right[2 * p, pl.ds(d, 16, stride=32), :]
            b = right[2 * p + 1, pl.ds(d, 16, stride=32), :]
            first = jnp.where(low_half, a, pltpu.roll(b, 64, 1))
            second = jnp.where(low_half, pltpu.roll(a, 64, 1), b)
            rows = pl.ds(pl.multiple_of(d * 32, 32), 32)
            high, low = split(jnp.concatenate([first, second], axis=0))
            lhs[rows, pl.ds(pl.multiple_of(p * 128, 128), 128)] = high
            lhs[rows, pl.ds(pl.multiple_of(512 + p * 128, 128), 128)] = low
            lhs[rows, pl.ds(pl.multiple_of(1024 + p * 128, 128), 128)] = high
            return carry

        lax.fori_loop(0, 32, body, 0, unroll=4)

    for at in range(9, 15):
        loads[at].wait()

    lane = lax.broadcasted_iota(jnp.int32, (32, 128), 1)
    below = lane < 64
    even = (lane // 32) % 2 == 0
    pbias, fbias, hbias = pbias_ref[...], fbias_ref[...], hbias_ref[...]
    pgain, poffset = pgain_ref[...], poffset_ref[...]

    def exchange_halves(a, b):
        moved = pltpu.roll(jnp.where(below, b, a), 64, 1)
        return jnp.where(below, a, moved), jnp.where(below, moved, b)

    def exchange_quarters(a, b):
        return jnp.where(even, a, pltpu.roll(b, 32, 1)), jnp.where(even, pltpu.roll(a, 96, 1), b)

    def outer(q):
        for h in range(2):
            high, low = split(left[q, h].reshape(512, 256))
            at = pl.ds(h * 256, 256)
            rhs[pl.ds(0, 512), at] = high
            rhs[pl.ds(512, 512), at] = high
            rhs[pl.ds(1024, 512), at] = low
        raw[q % 2] = dot(lhs[...], rhs[...])

    def finish(q):
        for t in range(8):
            for u in range(4):
                v = [raw[q % 2, pl.ds((4 * t + d) * 32, 32), pl.ds(u * 128, 128)] for d in range(4)]
                v[0], v[2] = exchange_halves(v[0], v[2])
                v[1], v[3] = exchange_halves(v[1], v[3])
                v[0], v[1] = exchange_quarters(v[0], v[1])
                v[2], v[3] = exchange_quarters(v[2], v[3])
                for i in range(4):
                    high, low = split(v[i])
                    oh[pl.ds((u * 4 + i) * 32, 32), pl.ds(t * 128, 128)] = high
                    ol[pl.ds((u * 4 + i) * 32, 32), pl.ds(t * 128, 128)] = low
        wide = dot(oh[...], pwc[...])
        update = wide[:, :128] + wide[:, 128:] + dot(ol[...], pwc[:, :128])
        tiles = [pl.ds((h * 32 + q * 8) * 32, 256) for h in range(2)]
        updated = jnp.concatenate([pair[rows, :] for rows in tiles], axis=0) + update * (1.0 / 512) + pbias
        (flat,) = center([updated], 128)
        high, low = split(flat * pgain + poffset)
        hidden = jnp.maximum(dot(jnp.concatenate([high, low, high], axis=1), hwc[...]) + hbias, 0.0)
        high, low = split(hidden)
        wide = dot(high, fwc[...])
        final = wide[:, :128] + wide[:, 128:] + dot(low, fwc[:, :128])
        result = updated + final + fbias
        for h in range(2):
            out[tiles[h], :] = result[h * 256 : h * 256 + 256]

    def store(q, h):
        rows = pl.ds(pl.multiple_of((h * 32 + q * 8) * 32, 256), 256)
        return pltpu.make_async_copy(out.at[rows, :], out_hbm.at[rows, :], out_sem.at[q * 2 + h])

    def arrive(q):
        for step in range(8):
            c_wait(step, q)

    def product(q):
        arrive(q)
        outer(q)

    def complete(q):
        finish(q)
        store(q, 0).start()
        store(q, 1).start()

    work = {
        "t1": swap_first,
        "t2": swap_second,
        "r0": right_relay(0, (3, 4)),
        "r1": right_relay(1, (5,)),
        "r4": right_relay(4, (6,)),
        "l0": left_relay(0, (3, 4)),
        "l1": left_relay(1, ()),
        "l2": left_relay(2, ()),
        "l3": left_relay(3, ()),
        "l4": left_relay(4, ()),
        "l5": left_relay(5, (6,)),
        "l6": left_relay(6, ()),
        "P": prepare,
        "O": product,
        "F": complete,
    }
    for name, n in ORDER:
        work[name](n)
    for n in range(CH):
        store(n, 0).wait()
        store(n, 1).wait()
    for n in range(CH):
        for step in range(7):
            r_copy(step, n, r_sent[step], r_to[step]).wait_send()
            l_sends(step, n).wait_send()
        for step in range(8):
            c_copy(step, n, c_slots[step], core).wait_send()

        @pl.when(jnp.logical_not(here_first))
        def _(n=n):
            first_copy(n).wait_send()

        @pl.when(jnp.logical_not(here_second))
        def _(n=n):
            second_copy(n).wait_send()


def on_device(
    alignment,
    align_gain,
    align_bias,
    left_weight,
    right_weight,
    project_weight,
    project_bias,
    pair_state,
    pair_gain,
    pair_bias,
    hidden_weight,
    hidden_bias,
    final_weight,
    final_bias,
):
    apart = pl.BlockSpec(memory_space=pl.ANY)
    dma = pltpu.SemaphoreType.DMA
    output = pl.pallas_call(
        kernel,
        out_shape=jax.ShapeDtypeStruct((2048, 128), F32),
        in_specs=[apart] * 14,
        out_specs=apart,
        scratch_shapes=[
            pltpu.VMEM((1, 256), F32),
            pltpu.VMEM((1, 256), F32),
            pltpu.VMEM((32, 256), F32),
            pltpu.VMEM((32, 256), F32),
            pltpu.VMEM((1, 128), F32),
            pltpu.VMEM((1, 128), F32),
            pltpu.VMEM((1, 128), F32),
            pltpu.VMEM((128, 512), F32),
            pltpu.VMEM((1, 512), F32),
            pltpu.VMEM((512, 128), F32),
            pltpu.VMEM((1, 128), F32),
            pltpu.VMEM((2048, 128), F32),
            pltpu.VMEM((2048, 128), F32),
            pltpu.VMEM((2, 256, 1024), BF16),
            pltpu.VMEM((2, 256, 1024), BF16),
            pltpu.VMEM((1024, 256), BF16),
            pltpu.VMEM((1024, 256), BF16),
            pltpu.VMEM((CH, 64, 256), F32),
            pltpu.VMEM((CH, 64, 256), F32),
            pltpu.VMEM((CH, 2, 8, 64, 256), F32),
            pltpu.VMEM((8, 512, 128), F32),
            pltpu.VMEM((1024, 1536), BF16),
            pltpu.VMEM((1536, 512), BF16),
            pltpu.VMEM((2, 1024, 512), F32),
            pltpu.VMEM((512, 1024), BF16),
            pltpu.VMEM((512, 1024), BF16),
            pltpu.VMEM((1024, 128), F32),
            pltpu.VMEM((1024, 256), BF16),
            pltpu.VMEM((384, 512), BF16),
            pltpu.VMEM((512, 256), BF16),
            pltpu.VMEM((2048, 128), F32),
            pltpu.VMEM((2048, 128), F32),
            dma((15,)),
            dma((7, CH)),
            dma((7, CH)),
            dma((7, CH)),
            dma((7, CH)),
            dma((8, CH)),
            dma((8, CH)),
            dma((2, CH)),
            dma((2, CH)),
            dma((8,)),
        ],
        compiler_params=pltpu.CompilerParams(
            collective_id=0, has_side_effects=True, vmem_limit_bytes=63 * 1024 * 1024
        ),
        cost_estimate=pl.CostEstimate(flops=10**10, bytes_accessed=6 * 10**6, transcendentals=0),
    )(
        alignment.reshape(2048, 256),
        align_gain.reshape(1, 256),
        align_bias.reshape(1, 256),
        left_weight.T,
        right_weight.T,
        project_weight,
        project_bias.reshape(1, 128),
        pair_state.reshape(2048, 128),
        pair_gain.reshape(1, 128),
        pair_bias.reshape(1, 128),
        hidden_weight,
        hidden_bias.reshape(1, 512),
        final_weight,
        final_bias.reshape(1, 128),
    )
    return output.reshape(64, 32, 128)


def solution(mesh):
    spread = P("row", "col", None)
    placed = (spread,) + (P(),) * 6 + (spread,) + (P(),) * 6
    return jax.shard_map(on_device, mesh=mesh, in_specs=placed, out_specs=spread, check_vma=False)
```
